256 devices in a mesh: ctx: 256 (over x, y, z, core).
Axes of the slice: x: 4, y: 4, z: 8, core: 2. Of those that a mesh axis runs over, the one named last changes fastest.
Arguments:
- queries: bfloat16 [131072, 1024], P('ctx'), may hold values from -6 to 6
- keys: bfloat16 [131072, 1024], P('ctx'), may hold values from -6 to 6
- values: bfloat16 [131072, 1024], P('ctx'), may hold values from -6 to 6
- out_grad: bfloat16 [131072, 1024], P('ctx'), may hold values from -6 to 6
Outputs:
- attended: bfloat16 [131072, 1024], P('ctx')
- query_grad: float32 [131072, 1024], P('ctx')
- key_grad: float32 [131072, 1024], P('ctx')
- value_grad: float32 [131072, 1024], P('ctx')
The draws below stay inside these ranges and needn't reach their ends.
All inputs are finite; a program needn't handle non-finite values.
Results may differ from the reference program's by a relative error of at most 0.011.
Values may be sent and summed in bfloat16 or wider, within the bound.
No kernel may reach another device: no remote copies, remote signals or barrier semaphores. Data moves between devices by JAX's collectives and lax.ppermute only.
A program may use at most 128 MiB of HBM per device.

```python
import math
import jax
import jax.numpy as jnp
from jax import lax

H = 8
HD = 128
NB = 128
LEVELS = 4
TOKENS = 131072


def draw_queries(key, part):
    key = jax.random.fold_in(key, 1)
    base_draw = jnp.clip(1.5 * jax.random.normal(key, (TOKENS, H * HD)), -6.0, 6.0)
    return base_draw.astype(jnp.bfloat16)


def draw_keys(key, part):
    key = jax.random.fold_in(key, 2)
    base_draw = jnp.clip(jax.random.normal(key, (TOKENS, H * HD)), -6.0, 6.0)
    return base_draw.astype(jnp.bfloat16)


def shard_levels(own_key, dims, split, smallest, high):
    factor_of, own = 1.0, jax.random.fold_in(own_key, 6)
    for position, parts in split:
        heights = jnp.exp(jax.random.uniform(jax.random.fold_in(own, position), (parts,), jnp.float32, smallest / len(split), high / len(split)))
        factor_of = factor_of * jnp.repeat(heights, dims[position] // parts).reshape([-1 if axis == position else 1 for axis in range(len(dims))])
    return factor_of


def normal_values(key, extent, deviation, reach, cuts=(), kind=jnp.bfloat16):
    values = deviation * jax.random.normal(key, extent, jnp.float32)
    if cuts:
        values = values * shard_levels(key, extent, cuts, -0.22, 0.18)
    return jnp.clip(values, -reach, reach).astype(kind)


def setup_inputs(seed: int = 0) -> dict:
    arg_keys = jax.random.split(jax.random.key(seed), 5)
    queries = draw_queries(jax.random.fold_in(arg_keys[4], 71), 0)
    keys = draw_keys(jax.random.fold_in(arg_keys[4], 71), 0)
    values = normal_values(arg_keys[2], (TOKENS, H * HD), 1.0, 6.0, ((0, 256),))
    out_grad = normal_values(arg_keys[3], (TOKENS, H * HD), 1.0, 6.0, ((0, 256),))
    return dict(queries=queries, keys=keys, values=values, out_grad=out_grad)


LN_TWO = math.log(2.0)

def pool_rows(matrix, factor):
    grouped = matrix.astype(jnp.float32).reshape(-1, factor, matrix.shape[-1])
    return lax.optimization_barrier(jnp.mean(grouped, axis=1)).astype(jnp.bfloat16)

def reference(queries, keys, values, out_grad):
    features = H * HD
    score_scale = 1.0 / math.sqrt(HD)
    padded_keys = []
    padded_vals = []
    level_rows = []
    for level_id in range(LEVELS):
        factor = 2 ** level_id
        if level_id == 0:
            key_pool = keys
            val_pool = values
        else:
            key_pool = pool_rows(keys, factor)
            val_pool = pool_rows(values, factor)
        padded_keys.append(jnp.pad(key_pool, ((NB, NB), (0, 0))))
        padded_vals.append(jnp.pad(val_pool, ((NB, NB), (0, 0))))
        level_rows.append(TOKENS // factor)

    def step(carry, block_id):
        key_acc, val_acc = carry
        first_row = block_id * NB
        q_rows = lax.dynamic_slice_in_dim(queries, first_row, NB, 0).astype(jnp.float32).reshape(NB, H, HD)
        g_rows = lax.dynamic_slice_in_dim(out_grad, first_row, NB, 0).astype(jnp.float32).reshape(NB, H, HD)
        key_parts = []
        val_parts = []
        bias_parts = []
        win_starts = []
        for level_id in range(LEVELS):
            span_tok = NB * 2 ** level_id
            super_no = first_row // span_tok
            win_start = (super_no * NB).astype(jnp.int32)
            win_starts.append(win_start)
            key_parts.append(lax.dynamic_slice_in_dim(padded_keys[level_id], win_start, 3 * NB, 0))
            val_parts.append(lax.dynamic_slice_in_dim(padded_vals[level_id], win_start, 3 * NB, 0))
            key_index = (super_no - 1) * NB + jnp.arange(3 * NB, dtype=jnp.int32)
            admitted = (key_index >= 0) & (key_index < level_rows[level_id])
            if level_id > 0:
                child_block = first_row // (span_tok // 2)
                admitted = admitted & (jnp.abs(key_index // (NB // 2) - child_block) > 1)
            bias_parts.append(jnp.where(admitted, jnp.float32(level_id * LN_TWO), jnp.float32(-jnp.inf)))
        k_all = jnp.concatenate(key_parts, axis=0).astype(jnp.float32).reshape(-1, H, HD)
        v_all = jnp.concatenate(val_parts, axis=0).astype(jnp.float32).reshape(-1, H, HD)
        key_bias = jnp.concatenate(bias_parts, axis=0)
        scores = jnp.einsum('qhd,khd->hqk', q_rows, k_all) * score_scale + key_bias[None, None, :]
        row_max = lax.optimization_barrier(jnp.max(scores, axis=-1, keepdims=True))
        exp_terms = jnp.exp(scores - row_max)
        prob_f32 = exp_terms / lax.optimization_barrier(jnp.sum(exp_terms, axis=-1, keepdims=True))
        attention_weight = lax.optimization_barrier(prob_f32.astype(jnp.bfloat16)).astype(jnp.float32)
        attended = jnp.einsum('hqk,khd->qhd', attention_weight, v_all).reshape(NB, features).astype(jnp.bfloat16)
        probability_gradient = jnp.einsum('qhd,khd->hqk', g_rows, v_all)
        row_delta = lax.optimization_barrier(jnp.sum(prob_f32 * probability_gradient, axis=-1, keepdims=True))
        logit_gradient = (prob_f32 * (probability_gradient - row_delta) * score_scale).astype(jnp.bfloat16)
        logit_gradient = lax.optimization_barrier(logit_gradient).astype(jnp.float32)
        q_grad = jnp.einsum('hqk,khd->qhd', logit_gradient, k_all).reshape(NB, features)
        k_grad = jnp.einsum('hqk,qhd->khd', logit_gradient, q_rows).reshape(-1, features)
        v_grad = jnp.einsum('hqk,qhd->khd', attention_weight, g_rows).reshape(-1, features)
        new_keys = []
        new_vals = []
        for level_id in range(LEVELS):
            lower_edge = level_id * 3 * NB
            old_key = lax.dynamic_slice_in_dim(key_acc[level_id], win_starts[level_id], 3 * NB, 0)
            old_val = lax.dynamic_slice_in_dim(val_acc[level_id], win_starts[level_id], 3 * NB, 0)
            new_keys.append(lax.dynamic_update_slice_in_dim(key_acc[level_id], old_key + k_grad[lower_edge:lower_edge + 3 * NB], win_starts[level_id], 0))
            new_vals.append(lax.dynamic_update_slice_in_dim(val_acc[level_id], old_val + v_grad[lower_edge:lower_edge + 3 * NB], win_starts[level_id], 0))
        return ((tuple(new_keys), tuple(new_vals)), (attended, q_grad))
    initial = (tuple((jnp.zeros((level_rows[l_id] + 2 * NB, features), jnp.float32) for l_id in range(LEVELS))), tuple((jnp.zeros((level_rows[l_id] + 2 * NB, features), jnp.float32) for l_id in range(LEVELS))))
    final_carry, stacked = lax.scan(step, initial, jnp.arange(TOKENS // NB, dtype=jnp.int32))
    key_acc, val_acc = final_carry
    attended = stacked[0].reshape(TOKENS, features)
    query_grad = stacked[1].reshape(TOKENS, features)
    key_grad = jnp.zeros((TOKENS, features), jnp.float32)
    value_grad = jnp.zeros((TOKENS, features), jnp.float32)
    for level_id in range(LEVELS):
        factor = 2 ** level_id
        key_grad = key_grad + jnp.repeat(key_acc[level_id][NB:-NB] / factor, factor, axis=0)
        value_grad = value_grad + jnp.repeat(val_acc[level_id][NB:-NB] / factor, factor, axis=0)
    return (attended, query_grad, key_grad, value_grad)
```

```python
import functools
import math

import jax
import jax.numpy as jnp
import numpy as np
from jax import lax
from jax.experimental import pallas as pl
from jax.experimental.pallas import tpu as pltpu
from jax.sharding import PartitionSpec as P

H = 8
HD = 128
NB = 128
HB = NB // 2
TOK = 4 * NB
EDGE = 2 * NB
ROWS = 9 * NB
SCALE = 1.0 / math.sqrt(HD)
SCALE_LOG2 = SCALE * math.log2(math.e)
PENALTY = 1e30
BF = jnp.bfloat16
F32 = jnp.float32


def pool_matrix(rows, source_rows, pieces):
    matrix = np.zeros((rows, source_rows), np.float32)
    for first, count, source, factor in pieces:
        for row in range(count):
            start = source + row * factor
            matrix[first + row, start : start + factor] = 1.0 / factor
    return matrix


BLOCK_POOL = pool_matrix(128, 128, [(0, 64, 0, 2), (64, 32, 0, 4), (96, 16, 0, 8)])
NEAR_POOL = pool_matrix(128, 256, [(0, 64, 0, 2), (64, 32, 0, 4), (96, 32, 128, 2)])
FAR_POOL = pool_matrix(64, 256, [(0, 16, 0, 8), (16, 16, 128, 4), (32, 32, 192, 2)])
SPREAD = pool_matrix(
    576,
    512,
    [
        (0, 128, 0, 1),
        (128, 64, 128, 2),
        (192, 64, 256, 4),
        (256, 128, 384, 1),
        (384, 64, 256, 2),
        (448, 64, 0, 4),
        (512, 64, 0, 8),
    ],
).T
BLOCK_SPREAD = np.concatenate([BLOCK_POOL[:64].T, BLOCK_POOL[:64].T], axis=1)


def mm(a, b):
    return jnp.dot(a, b, preferred_element_type=F32)


def mm_nt(a, b):
    return lax.dot_general(a, b, (((1,), (1,)), ((), ())), preferred_element_type=F32)


def is_even():
    return lax.rem(lax.axis_index("ctx"), 2) == 0


def pool_kernel(pool_ref, k_ref, v_ref, cross_ref, inner_ref, far_ref):
    even = is_even()
    for which, ref in enumerate((k_ref, v_ref)):
        pooled = [
            mm(pool_ref[...], ref[b * NB : (b + 1) * NB, :]).astype(BF) for b in range(4)
        ]

        def left(out):
            out[which, :NB] = ref[:NB, :]
            out[which, NB : NB + 64] = pooled[1][:64]
            out[which, NB + 64 : NB + 96] = pooled[2][64:96]
            out[which, NB + 96 :] = pooled[3][64:96]

        def right(out):
            out[which, :NB] = ref[3 * NB :, :]
            out[which, NB : NB + 64] = pooled[2][:64]
            out[which, NB + 64 : NB + 96] = pooled[0][64:96]
            out[which, NB + 96 :] = pooled[1][64:96]

        @pl.when(even)
        def _():
            left(cross_ref)
            right(inner_ref)

        @pl.when(jnp.logical_not(even))
        def _():
            right(cross_ref)
            left(inner_ref)

        for b in range(4):
            far_ref[which, b * 16 : (b + 1) * 16] = pooled[b][96:112]


def far_kernel(pool_ref, cross_ref, far_ref, out_ref):
    for which in range(2):
        out_ref[which, :64] = far_ref[which]
        out_ref[which, 64:] = mm(pool_ref[...], cross_ref[which]).astype(BF)


def fold_kernel(pool_ref, cross_ref, far_ref, got_ref, cross_out, far_out):
    for which in range(2):
        spread = mm(pool_ref[...], got_ref[which, 64:])
        cross_out[which] = (cross_ref[which].astype(F32) + spread).astype(BF)
        far_out[which] = (far_ref[which].astype(F32) + got_ref[which, :64].astype(F32)).astype(BF)


def final_kernel(spread_ref, cross_ref, inner_ref, far_ref, kg_ref, vg_ref, kg_out, vg_out):
    even = is_even()
    for which, (ref, out) in enumerate(((kg_ref, kg_out), (vg_ref, vg_out))):
        cross = cross_ref[which]
        inner = inner_ref[which]
        left = jnp.where(even, cross, inner)
        right = jnp.where(even, inner, cross)
        rows = jnp.concatenate([left, right, far_ref[which]], axis=0)
        out[...] = ref[...] + mm(spread_ref[...], rows)


PAIR_ROWS = (
    ((0, 384), (512, 704), (768, 1152)),
    ((128, 512), (576, 768), (768, 1152)),
)
PAIR_ZEROS = (((384, 512), (704, 768)), ((0, 128), (512, 576)))
CHUNKS = (
    (
        (0, 128, 0, "left"),
        (128, 512, 0, "own"),
        (512, 576, 1, "own"),
        (576, 640, 1, "left"),
        (640, 704, 1, "own"),
        (704, 768, 1, "left"),
        (768, 832, 2, "left"),
        (832, 960, 2, "right"),
        (960, 1024, 3, "far0"),
        (1024, 1088, 3, "far1"),
        (1088, 1152, 3, "far2"),
    ),
    (
        (0, 384, 0, "own"),
        (384, 512, 0, "right"),
        (512, 576, 1, "right"),
        (576, 640, 1, "own"),
        (640, 704, 1, "right"),
        (704, 768, 1, "own"),
        (768, 896, 2, "left"),
        (896, 960, 2, "right"),
        (960, 1024, 3, "far0"),
        (1024, 1088, 3, "far1"),
        (1088, 1152, 3, "far2"),
    ),
)


def overlap(chunk, ranges):
    for low, high in ranges:
        first, end = max(chunk[0], low), min(chunk[1], high)
        if first < end:
            return first, end
    return None


def fold_rows(x, op):
    return op(x.reshape(x.shape[0] // 8, 8, x.shape[1]), axis=0)


def core_kernel(
    devices,
    pool_ref,
    near_ref,
    near_t_ref,
    spread_ref,
    q_ref,
    k_ref,
    v_ref,
    g_ref,
    cross_ref,
    inner_ref,
    far_ref,
    swap_ref,
    att_ref,
    dq_ref,
    kg_ref,
    vg_ref,
    crossg_ref,
    innerg_ref,
    farg_ref,
    swapg_ref,
    rows_ref,
    cols_ref,
    s_ref,
    p_ref,
    ds_ref,
):
    d = lax.axis_index("ctx")
    even = is_even()

    def penalty(valid):
        return jnp.where(valid, 0.0, PENALTY).astype(F32)

    step = jnp.where(even, 1, -1)
    far_ids = (d - 2 * step, d + 3 * step, d + 2 * step)
    penalties = {"own": 0.0, "left": penalty(d > 0), "right": penalty(d < devices - 1)}
    for i, far_id in enumerate(far_ids):
        penalties["far%d" % i] = penalty((far_id >= 0) & (far_id < devices))

    @pl.when(pl.program_id(0) == 0)
    def _():
        for pair in range(2):
            for blk in range(2):
                for low, high in PAIR_ZEROS[blk]:
                    zeros = jnp.zeros((high - low, NB), BF)
                    p_ref[pair, low:high, blk * NB : (blk + 1) * NB] = zeros
                    ds_ref[pair, low:high, blk * NB : (blk + 1) * NB] = zeros

    for which, own in enumerate((k_ref, v_ref)):
        cross = cross_ref[which]
        inner = inner_ref[which]
        left = jnp.where(even, cross, inner)
        right = jnp.where(even, inner, cross)
        near_l = mm(near_ref[...], left).astype(BF)
        near_r = mm(near_ref[...], right).astype(BF)
        halves = [
            mm(pool_ref[:64], own[b * NB : (b + 1) * NB, :]).astype(BF) for b in range(4)
        ]
        a = rows_ref.at[0, which]
        b = rows_ref.at[1, which]
        a[:128] = left[:128]
        a[128:512] = own[: 3 * NB, :]
        a[512:576] = halves[2]
        a[576:640] = left[128:192]
        a[640:704] = halves[3]
        a[704:768] = near_l[:64]
        a[768:832] = left[192:256]
        a[832:896] = near_r[64:]
        a[896:960] = right[192:256]
        b[:384] = own[NB:, :]
        b[384:512] = right[:128]
        b[512:576] = near_r[:64]
        b[576:640] = halves[0]
        b[640:704] = right[128:192]
        b[704:768] = halves[1]
        b[768:832] = left[192:256]
        b[832:896] = near_l[64:]
        b[896:960] = right[192:256]
        for pair in (a, b):
            pair[960:1024] = far_ref[which]
            pair[1024:1152] = swap_ref[which]
        for pair in range(2):
            cols_ref[pair, which] = rows_ref[pair, which].T

    grads = []
    for pair in range(2):
        first = pair * 2 * NB
        q = q_ref[first : first + 2 * NB, :]
        g = g_ref[first : first + 2 * NB, :]
        g_t = g.T
        best = [None, None]
        for chunk in CHUNKS[pair]:
            low, high, level, side = chunk
            s = mm_nt(rows_ref[pair, 0, low:high], q)
            s_ref[pair, low:high] = s
            for blk in range(2):
                part = overlap(chunk, PAIR_ROWS[blk])
                if part is None:
                    continue
                piece = s[part[0] - low : part[1] - low, blk * NB : (blk + 1) * NB]
                top = fold_rows(piece, jnp.max) * SCALE_LOG2 + (level - penalties[side])
                best[blk] = top if best[blk] is None else jnp.maximum(best[blk], top)
        best = [jnp.max(b, axis=0, keepdims=True) for b in best]
        totals = []
        for blk in range(2):
            lanes = slice(blk * NB, (blk + 1) * NB)
            total = jnp.zeros((8, NB), F32)
            for chunk in CHUNKS[pair]:
                low, high, level, side = chunk
                part = overlap(chunk, PAIR_ROWS[blk])
                if part is None:
                    continue
                shift = best[blk] - (level - penalties[side])
                prob = jnp.exp2(s_ref[pair, part[0] : part[1], lanes] * SCALE_LOG2 - shift)
                total = total + fold_rows(prob, jnp.sum)
                p_ref[pair, part[0] : part[1], lanes] = prob.astype(BF)
            totals.append(jnp.sum(total, axis=0, keepdims=True))
        inverse = 1.0 / jnp.concatenate(totals, axis=1)
        out_t = mm(cols_ref[pair, 1], p_ref[pair]) * inverse
        att_ref[first : first + 2 * NB, :] = out_t.T.astype(BF)
        delta = jnp.sum(out_t * g_t.astype(F32), axis=0, keepdims=True)
        for chunk in CHUNKS[pair]:
            low, high, level, side = chunk
            dp = mm(rows_ref[pair, 1, low:high], g_t)
            for blk in range(2):
                lanes = slice(blk * NB, (blk + 1) * NB)
                part = overlap(chunk, PAIR_ROWS[blk])
                if part is None:
                    continue
                piece = dp[part[0] - low : part[1] - low, lanes]
                prob = p_ref[pair, part[0] : part[1], lanes].astype(F32) * inverse[:, lanes]
                p_ref[pair, part[0] : part[1], lanes] = prob.astype(BF)
                ds_ref[pair, part[0] : part[1], lanes] = (
                    prob * (piece - delta[:, lanes])
                ).astype(BF)
        dq_t = mm(cols_ref[pair, 0], ds_ref[pair]) * SCALE
        dq_ref[first : first + 2 * NB, :] = dq_t.T
        grads.append((mm(ds_ref[pair], q) * SCALE, mm(p_ref[pair], g)))

    for which, out in enumerate((kg_ref, vg_ref)):
        a = grads[0][which]
        b = grads[1][which]
        tokens = (
            a[128:256],
            a[256:384] + b[:128],
            a[384:512] + b[128:256],
            b[256:384],
        )
        halves = (b[576:640], b[704:768], a[512:576], a[640:704])
        for blk in range(4):
            high = halves[blk].astype(BF)
            low = (halves[blk] - high.astype(F32)).astype(BF)
            spread = mm(spread_ref[...], jnp.concatenate([high, low], axis=0))
            out[blk * NB : (blk + 1) * NB, :] = tokens[blk] + spread
        near_l = jnp.concatenate([a[704:768], b[832:896]], axis=0).astype(BF)
        near_r = jnp.concatenate([b[512:576], a[832:896]], axis=0).astype(BF)
        left = jnp.concatenate([a[:128], a[576:640], a[768:832] + b[768:832]], axis=0)
        right = jnp.concatenate([b[384:512], b[640:704], a[896:960] + b[896:960]], axis=0)
        left = (left + mm(near_t_ref[...], near_l)).astype(BF)
        right = (right + mm(near_t_ref[...], near_r)).astype(BF)
        crossg_ref[which] = jnp.where(even, left, right)
        innerg_ref[which] = jnp.where(even, right, left)
        far = (a[960:] + b[960:]).astype(BF)
        farg_ref[which] = far[:64]
        swapg_ref[which] = far[64:]


VMEM_LIMIT = 56 * 2**20


def params():
    return pltpu.CompilerParams(vmem_limit_bytes=VMEM_LIMIT)


def whole(shape):
    return pl.BlockSpec(shape, lambda i: (0,) * len(shape))


def lanes(rows, width, pair=True):
    if pair:
        return pl.BlockSpec((2, rows, width), lambda i: (0, 0, i))
    return pl.BlockSpec((rows, width), lambda i: (0, i))


def constant(matrix):
    return jnp.asarray(matrix, BF)


def shaped(*shape, dtype=BF):
    return jax.ShapeDtypeStruct(shape, dtype)


def swap_pairs(n):
    return [(i, i ^ 1) for i in range(n)]


def in_range(pairs, n):
    return [(i, j) for i, j in pairs if 0 <= j < n]


def cross_pairs(n):
    return in_range([(i, i + 1 if i % 2 else i - 1) for i in range(n)], n)


def far_pairs(n):
    return in_range([(i, i - 2 if i % 2 else i + 2) for i in range(n)], n)


def back_pairs(n):
    return in_range([(i, i + 2 if i % 2 else i - 2) for i in range(n)], n)


def body(queries, keys, values, out_grad):
    tok, feat = queries.shape
    n = lax.axis_size("ctx")
    width = 256
    cross, inner, far = pl.pallas_call(
        pool_kernel,
        grid=(feat // width,),
        in_specs=[whole((128, 128)), lanes(tok, width, False), lanes(tok, width, False)],
        out_specs=[lanes(EDGE, width), lanes(EDGE, width), lanes(64, width)],
        out_shape=[shaped(2, EDGE, feat), shaped(2, EDGE, feat), shaped(2, 64, feat)],
        compiler_params=params(),
        name="pool",
    )(constant(BLOCK_POOL), keys, values)
    cross_in = lax.ppermute(cross, "ctx", cross_pairs(n))
    far_in = lax.ppermute(far, "ctx", far_pairs(n))
    inner_in = lax.ppermute(inner, "ctx", swap_pairs(n))
    far_send = pl.pallas_call(
        far_kernel,
        grid=(feat // width,),
        in_specs=[whole((64, 256)), lanes(EDGE, width), lanes(64, width)],
        out_specs=lanes(128, width),
        out_shape=shaped(2, 128, feat),
        compiler_params=params(),
        name="far",
    )(constant(FAR_POOL), cross_in, far_in)
    swap_in = lax.ppermute(far_send, "ctx", swap_pairs(n))

    att, dq, kg, vg, cross_g, inner_g, far_g, swap_g = pl.pallas_call(
        functools.partial(core_kernel, n),
        grid=(feat // HD,),
        in_specs=[
            whole((128, 128)),
            whole((128, 256)),
            whole((256, 128)),
            whole((128, 128)),
            lanes(tok, HD, False),
            lanes(tok, HD, False),
            lanes(tok, HD, False),
            lanes(tok, HD, False),
            lanes(EDGE, HD),
            lanes(EDGE, HD),
            lanes(64, HD),
            lanes(128, HD),
        ],
        out_specs=[
            lanes(tok, HD, False),
            lanes(tok, HD, False),
            lanes(tok, HD, False),
            lanes(tok, HD, False),
            lanes(EDGE, HD),
            lanes(EDGE, HD),
            lanes(64, HD),
            lanes(128, HD),
        ],
        out_shape=[
            shaped(tok, feat),
            shaped(tok, feat, dtype=F32),
            shaped(tok, feat, dtype=F32),
            shaped(tok, feat, dtype=F32),
            shaped(2, EDGE, feat),
            shaped(2, EDGE, feat),
            shaped(2, 64, feat),
            shaped(2, 128, feat),
        ],
        scratch_shapes=[
            pltpu.VMEM((2, 2, ROWS, HD), BF),
            pltpu.VMEM((2, 2, HD, ROWS), BF),
            pltpu.VMEM((2, ROWS, 2 * NB), F32),
            pltpu.VMEM((2, ROWS, 2 * NB), BF),
            pltpu.VMEM((2, ROWS, 2 * NB), BF),
        ],
        compiler_params=params(),
        name="core",
    )(
        constant(BLOCK_POOL),
        constant(NEAR_POOL),
        constant(NEAR_POOL.T),
        constant(BLOCK_SPREAD),
        queries,
        keys,
        values,
        out_grad,
        cross_in,
        inner_in,
        far_in,
        swap_in,
    )

    swap_back = lax.ppermute(swap_g, "ctx", swap_pairs(n))
    cross_g, far_g = pl.pallas_call(
        fold_kernel,
        grid=(feat // width,),
        in_specs=[whole((256, 64)), lanes(EDGE, width), lanes(64, width), lanes(128, width)],
        out_specs=[lanes(EDGE, width), lanes(64, width)],
        out_shape=[shaped(2, EDGE, feat), shaped(2, 64, feat)],
        compiler_params=params(),
        name="fold",
    )(constant(FAR_POOL.T), cross_g, far_g, swap_back)
    cross_back = lax.ppermute(cross_g, "ctx", cross_pairs(n))
    far_back = lax.ppermute(far_g, "ctx", back_pairs(n))
    inner_back = lax.ppermute(inner_g, "ctx", swap_pairs(n))
    kg, vg = pl.pallas_call(
        final_kernel,
        grid=(feat // width,),
        in_specs=[
            whole((512, 576)),
            lanes(EDGE, width),
            lanes(EDGE, width),
            lanes(64, width),
            lanes(tok, width, False),
            lanes(tok, width, False),
        ],
        out_specs=[lanes(tok, width, False), lanes(tok, width, False)],
        out_shape=[shaped(tok, feat, dtype=F32), shaped(tok, feat, dtype=F32)],
        input_output_aliases={4: 0, 5: 1},
        compiler_params=params(),
        name="final",
    )(constant(SPREAD), cross_back, inner_back, far_back, kg, vg)
    return att, dq, kg, vg


def solution(mesh):
    spec = P("ctx", None)
    return jax.shard_map(
        body,
        mesh=mesh,
        in_specs=(spec, spec, spec, spec),
        out_specs=(spec, spec, spec, spec),
        check_vma=False,
    )
```

```python
import functools
import math

import jax
import jax.numpy as jnp
import numpy as np
from jax import lax
from jax.experimental import pallas as pl
from jax.experimental.pallas import tpu as pltpu
from jax.sharding import PartitionSpec as P

HD = 128
NB = 128
PAIR = 2 * NB
EDGE = 2 * NB
SCALE = 1.0 / math.sqrt(HD)
SCALE_LOG2 = SCALE * math.log2(math.e)
PENALTY = 1e30
BF = jnp.bfloat16
F32 = jnp.float32


def pool_matrix(rows, source_rows, pieces):
    matrix = np.zeros((rows, source_rows), np.float32)
    for first, count, source, factor in pieces:
        for row in range(count):
            start = source + row * factor
            matrix[first + row, start : start + factor] = 1.0 / factor
    return matrix


BLOCK_POOL = pool_matrix(64, 128, [(0, 64, 0, 2)])
NEAR_POOL = pool_matrix(128, 256, [(0, 64, 0, 2), (64, 32, 0, 4), (96, 32, 128, 2)])
FAR_POOL = pool_matrix(64, 256, [(0, 16, 0, 8), (16, 16, 128, 4), (32, 32, 192, 2)])
SPREAD = pool_matrix(
    576,
    512,
    [
        (0, 128, 0, 1),
        (128, 64, 128, 2),
        (192, 64, 256, 4),
        (256, 128, 384, 1),
        (384, 64, 256, 2),
        (448, 64, 0, 4),
        (512, 64, 0, 8),
    ],
).T
BLOCK_SPREAD = np.concatenate([BLOCK_POOL.T, BLOCK_POOL.T], axis=1)


def mm(a, b):
    return jnp.dot(a, b, preferred_element_type=F32)


def mm_nt(a, b):
    return lax.dot_general(a, b, (((1,), (1,)), ((), ())), preferred_element_type=F32)


def is_even():
    return lax.rem(lax.axis_index("ctx"), 2) == 0


def block(even, number):
    return pl.ds(pl.multiple_of(jnp.where(even, number, 3 - number) * NB, NB), NB)


def pool_kernel(k_ref, v_ref, cross_ref, inner_ref, far_ref):
    even = is_even()
    row = lax.broadcasted_iota(jnp.int32, (NB, NB), 0)
    col = lax.broadcasted_iota(jnp.int32, (NB, NB), 1)
    matrix = jnp.where(row == (col >> 1), 0.5, 0.0)
    matrix = jnp.where(row == (col >> 2) + 64, 0.25, matrix)
    matrix = jnp.where(row == (col >> 3) + 96, 0.125, matrix).astype(BF)
    for which, ref in enumerate((k_ref, v_ref)):
        pooled = [mm(matrix, ref[block(even, b), :]).astype(BF) for b in range(4)]
        cross_ref[which, :128] = ref[block(even, 0), :]
        cross_ref[which, 128:192] = pooled[1][:64]
        cross_ref[which, 192:224] = pooled[2][64:96]
        cross_ref[which, 224:] = pooled[3][64:96]
        inner_ref[which, :128] = ref[block(even, 3), :]
        inner_ref[which, 128:192] = pooled[2][:64]
        inner_ref[which, 192:224] = pooled[0][64:96]
        inner_ref[which, 224:] = pooled[1][64:96]
        for b in range(4):
            far_ref[which, b * 16 : (b + 1) * 16] = pooled[b][96:112]


def far_kernel(pool_ref, cross_ref, far_ref, out_ref):
    for which in range(2):
        out_ref[which, :64] = far_ref[which]
        out_ref[which, 64:] = mm(pool_ref[...], cross_ref[which]).astype(BF)


def fold_kernel(pool_ref, cross_ref, far_ref, got_ref, cross_out, far_out):
    for which in range(2):
        spread = mm(pool_ref[...], got_ref[which, 64:])
        cross_out[which] = (cross_ref[which].astype(F32) + spread).astype(BF)
        far_out[which] = (far_ref[which].astype(F32) + got_ref[which, :64].astype(F32)).astype(BF)


def final_kernel(spread_ref, cross_ref, inner_ref, far_ref, kg_ref, vg_ref, kg_out, vg_out):
    even = is_even()
    for which, (ref, out) in enumerate(((kg_ref, kg_out), (vg_ref, vg_out))):
        rows = jnp.concatenate([cross_ref[which], inner_ref[which], far_ref[which]], axis=0)
        spread = mm(spread_ref[...], rows)
        for b in range(4):
            at = block(even, b)
            out[at, :] = ref[at, :].astype(F32) + spread[b * NB : (b + 1) * NB]


NEAR_ROWS = (640, 832)
NEAR_CHUNKS = (
    ((0, 384, 0, "own"), (384, 512, 1, "own"), (512, 640, 2, "inner")),
    (
        (0, 384, 0, "own"),
        (384, 512, 0, "inner"),
        (512, 576, 1, "inner"),
        (576, 640, 1, "own"),
        (640, 704, 1, "inner"),
        (704, 768, 1, "own"),
        (768, 832, 2, "inner"),
    ),
)
NEAR_ADMIT = (
    (((0, 256), (384, 512), (512, 640)), ((0, 384), (448, 512), (512, 640))),
    (((0, 384), (512, 704), (768, 832)), ((128, 512), (576, 768), (768, 832))),
)
NEAR_ZEROS = (
    (((256, 384),), ((384, 448),)),
    (((384, 512), (704, 768)), ((0, 128), (512, 576))),
)
CROSS_ROWS = 640
CROSS_SPAN = ((0, 512), (256, 576))
CROSS_CHUNKS = (
    (
        (0, 128, 0, "cross"),
        (128, 192, 1, "cross"),
        (192, 256, 1, "cross"),
        (256, 320, 2, "cross"),
        (320, 384, 3, "far0"),
        (384, 448, 3, "far1"),
        (448, 512, 3, "far2"),
    ),
    (
        (256, 320, 2, "cross"),
        (320, 384, 3, "far0"),
        (384, 448, 3, "far1"),
        (448, 512, 3, "far2"),
        (512, 576, 2, "cross"),
    ),
)
CROSS_ADMIT = ((((0, 128), (192, 512)), ((128, 512),)), (((256, 576),), ((256, 576),)))
CROSS_ZEROS = ((((128, 192),), ((0, 128),)), ((), ()))


def overlap(chunk, ranges):
    for low, high in ranges:
        first, end = max(chunk[0], low), min(chunk[1], high)
        if first < end:
            return first, end
    return None


def fold_rows(x, op):
    return op(x.reshape(x.shape[0] // 8, 8, x.shape[1]), axis=0)


def lanes_of(blk):
    return slice(blk * NB, (blk + 1) * NB)


def penalties_of(devices):
    d = lax.axis_index("ctx")
    step = jnp.where(is_even(), 1, -1)

    def penalty(other):
        return jnp.where((other >= 0) & (other < devices), 0.0, PENALTY).astype(F32)

    return {
        "own": 0.0,
        "cross": penalty(d - step),
        "inner": penalty(d + step),
        "far0": penalty(d - 2 * step),
        "far1": penalty(d + 3 * step),
        "far2": penalty(d + 2 * step),
    }


def scores(chunks, admit, penalties, rows, q, s_ref):
    best = [None, None]
    for chunk in chunks:
        low, high, level, side = chunk
        s = mm_nt(rows[low:high], q)
        s_ref[low:high] = s
        for blk in range(2):
            part = overlap(chunk, admit[blk])
            if part is None:
                continue
            piece = s[part[0] - low : part[1] - low, lanes_of(blk)]
            top = fold_rows(piece, jnp.max) * SCALE_LOG2 + (level - penalties[side])
            best[blk] = top if best[blk] is None else jnp.maximum(best[blk], top)
    return jnp.concatenate([jnp.max(b, axis=0, keepdims=True) for b in best], axis=1)


def exponentials(chunks, admit, penalties, best, s_ref, p_ref, base):
    totals = []
    for blk in range(2):
        lanes = lanes_of(blk)
        total = jnp.zeros((8, NB), F32)
        for chunk in chunks:
            low, high, level, side = chunk
            part = overlap(chunk, admit[blk])
            if part is None:
                continue
            shift = best[:, lanes] - (level - penalties[side])
            prob = jnp.exp2(s_ref[part[0] : part[1], lanes] * SCALE_LOG2 - shift)
            total = total + fold_rows(prob, jnp.sum)
            p_ref[part[0] - base : part[1] - base, lanes] = prob.astype(BF)
        totals.append(jnp.sum(total, axis=0, keepdims=True))
    return jnp.concatenate(totals, axis=1)


def score_grads(chunks, admit, rows, g_t, inverse, delta, exp_ref, p_ref, ds_ref, base):
    for chunk in chunks:
        low, high, level, side = chunk
        dp = mm(rows[low:high], g_t)
        for blk in range(2):
            lanes = lanes_of(blk)
            part = overlap(chunk, admit[blk])
            if part is None:
                continue
            here = slice(part[0] - base, part[1] - base)
            piece = dp[part[0] - low : part[1] - low, lanes]
            prob = exp_ref[here, lanes].astype(F32) * inverse[:, lanes]
            p_ref[here, lanes] = prob.astype(BF)
            ds_ref[here, lanes] = (prob * (piece - delta[:, lanes])).astype(BF)


def put_zeros(zeros, base, *refs):
    for ref in refs:
        for blk in range(2):
            for low, high in zeros[blk]:
                ref[low - base : high - base, lanes_of(blk)] = jnp.zeros((high - low, NB), BF)


def lay_near(even, which, own, inner_ref, pool_ref, near_ref, a, b):
    inner = inner_ref[which]
    near = mm(near_ref[...], inner).astype(BF)
    tokens = [own[block(even, i), :] for i in range(4)]
    halves = [mm(pool_ref[...], t).astype(BF) for t in tokens]
    a[:128] = tokens[0]
    a[128:256] = tokens[1]
    a[256:384] = tokens[2]
    a[384:448] = halves[2]
    a[448:512] = halves[3]
    a[512:576] = near[64:]
    a[576:640] = inner[192:]
    b[:128] = tokens[1]
    b[128:256] = tokens[2]
    b[256:384] = tokens[3]
    b[384:512] = inner[:128]
    b[512:576] = near[:64]
    b[576:640] = halves[0]
    b[640:704] = inner[128:192]
    b[704:768] = halves[1]
    b[768:832] = inner[192:]


STEP = 2
WIDE = STEP * HD
UNITS = tuple((head, pair) for head in range(STEP) for pair in range(2))


def two(even, ref, pair, head):
    lanes = lanes_of(head)
    return jnp.concatenate(
        [ref[block(even, 2 * pair), lanes], ref[block(even, 2 * pair + 1), lanes]], axis=0
    )


def put_two(even, ref, pair, head, rows):
    ref[block(even, 2 * pair), lanes_of(head)] = rows[:NB]
    ref[block(even, 2 * pair + 1), lanes_of(head)] = rows[NB:]


def staggered(*stages):
    for time in range(len(UNITS) + len(stages) - 1):
        for lag, stage in enumerate(stages):
            if 0 <= time - lag < len(UNITS):
                stage(*UNITS[time - lag])


def columns(pair):
    return slice(pair * PAIR, (pair + 1) * PAIR)


def first_kernel(
    devices,
    pool_ref,
    near_ref,
    q_ref,
    k_ref,
    v_ref,
    inner_ref,
    pa_ref,
    pb_ref,
    out_ref,
    stat_ref,
    ka_ref,
    kb_ref,
    va_ref,
    vb_ref,
    s_ref,
):
    even = is_even()
    penalties = penalties_of(devices)
    lay_near(even, 0, k_ref, inner_ref, pool_ref, near_ref, ka_ref, kb_ref)
    lay_near(even, 1, v_ref, inner_ref, pool_ref, near_ref, va_ref, vb_ref)
    keys, values, exps = (ka_ref, kb_ref), (va_ref, vb_ref), (pa_ref, pb_ref)
    best = {}

    def score(head, pair):
        best[head, pair] = scores(
            NEAR_CHUNKS[pair],
            NEAR_ADMIT[pair],
            penalties,
            keys[pair].at[:, lanes_of(head)],
            two(even, q_ref, pair, head),
            s_ref.at[head, pair],
        )

    def exponential(head, pair):
        p = exps[pair].at[head]
        put_zeros(NEAR_ZEROS[pair], 0, p)
        total = exponentials(
            NEAR_CHUNKS[pair],
            NEAR_ADMIT[pair],
            penalties,
            best[head, pair],
            s_ref.at[head, pair],
            p,
            0,
        )
        stat_ref[head, 0:1, columns(pair)] = best[head, pair]
        stat_ref[head, 1:2, columns(pair)] = total

    def attend(head, pair):
        cols = values[pair][:, lanes_of(head)].T
        out_ref[head, :, columns(pair)] = mm(cols, exps[pair][head])

    staggered(score, exponential, attend)


def cross_kernel(
    devices,
    near_ref,
    near_t_ref,
    q_ref,
    g_ref,
    cross_ref,
    far_ref,
    swap_ref,
    sum_ref,
    stat_ref,
    att_ref,
    dq_ref,
    stat_out,
    crossg_ref,
    farg_ref,
    swapg_ref,
    k_ref,
    v_ref,
    s_ref,
    p_ref,
    ds_ref,
):
    even = is_even()
    penalties = penalties_of(devices)

    @pl.when(pl.program_id(0) == 0)
    def _():
        for head, pair in UNITS:
            base = CROSS_SPAN[pair][0]
            put_zeros(CROSS_ZEROS[pair], base, p_ref.at[head, pair], ds_ref.at[head, pair])

    for which, rows in enumerate((k_ref, v_ref)):
        cross = cross_ref[which]
        near = mm(near_ref[...], cross).astype(BF)
        rows[:128] = cross[:128]
        rows[128:192] = near[:64]
        rows[192:256] = cross[128:192]
        rows[256:320] = cross[192:]
        rows[320:384] = far_ref[which]
        rows[384:512] = swap_ref[which]
        rows[512:576] = near[64:]
        rows[576:] = jnp.zeros((64, WIDE), BF)
    state = {}
    grads = {}

    def score(head, pair):
        best = scores(
            CROSS_CHUNKS[pair],
            CROSS_ADMIT[pair],
            penalties,
            k_ref.at[:, lanes_of(head)],
            two(even, q_ref, pair, head),
            s_ref.at[head, pair],
        )
        state[head, pair] = jnp.maximum(best, stat_ref[head, 0:1, columns(pair)])

    def exponential(head, pair):
        best = state[head, pair]
        total = exponentials(
            CROSS_CHUNKS[pair],
            CROSS_ADMIT[pair],
            penalties,
            best,
            s_ref.at[head, pair],
            p_ref.at[head, pair],
            CROSS_SPAN[pair][0],
        )
        factor = jnp.exp2(stat_ref[head, 0:1, columns(pair)] - best)
        inverse = 1.0 / (total + stat_ref[head, 1:2, columns(pair)] * factor)
        state[head, pair] = factor, inverse

    def attend(head, pair):
        base, end = CROSS_SPAN[pair]
        factor, inverse = state[head, pair]
        cols = v_ref[base:end, lanes_of(head)].T
        new = mm(cols, p_ref[head, pair, : end - base])
        out_t = (sum_ref[head, :, columns(pair)] * factor + new) * inverse
        put_two(even, att_ref, pair, head, out_t.T.astype(BF))
        g_t = two(even, g_ref, pair, head).T
        delta = jnp.sum(out_t * g_t.astype(F32), axis=0, keepdims=True)
        stat_out[head, 0:1, columns(pair)] = inverse * factor
        stat_out[head, 1:2, columns(pair)] = delta
        state[head, pair] = inverse, delta, g_t

    def differentiate(head, pair):
        inverse, delta, g_t = state[head, pair]
        p = p_ref.at[head, pair]
        score_grads(
            CROSS_CHUNKS[pair],
            CROSS_ADMIT[pair],
            v_ref.at[:, lanes_of(head)],
            g_t,
            inverse,
            delta,
            p,
            p,
            ds_ref.at[head, pair],
            CROSS_SPAN[pair][0],
        )

    def multiply(head, pair):
        base, end = CROSS_SPAN[pair]
        ds = ds_ref[head, pair, : end - base]
        cols = k_ref[base:end, lanes_of(head)].T
        dq_ref[head, :, columns(pair)] = mm(cols, ds)
        grads[head, pair] = (
            mm(ds, two(even, q_ref, pair, head)) * SCALE,
            mm(p_ref[head, pair, : end - base], two(even, g_ref, pair, head)),
        )

    staggered(score, exponential, attend, differentiate, multiply)
    for head in range(STEP):
        lanes = lanes_of(head)
        for which in range(2):
            a = grads[head, 0][which]
            b = grads[head, 1][which]
            near = jnp.concatenate([a[128:192], b[256:320]], axis=0).astype(BF)
            edge = jnp.concatenate([a[:128], a[192:256], a[256:320] + b[:64]], axis=0)
            crossg_ref[which, :, lanes] = (edge + mm(near_t_ref[...], near)).astype(BF)
            far = (a[320:512] + b[64:256]).astype(BF)
            farg_ref[which, :, lanes] = far[:64]
            swapg_ref[which, :, lanes] = far[64:]


def last_kernel(
    pool_ref,
    near_ref,
    near_t_ref,
    spread_ref,
    q_ref,
    k_ref,
    v_ref,
    g_ref,
    inner_ref,
    pa_ref,
    pb_ref,
    stat_ref,
    dqt_ref,
    dq_ref,
    kg_ref,
    vg_ref,
    innerg_ref,
    ka_ref,
    kb_ref,
    va_ref,
    vb_ref,
    wa_ref,
    wb_ref,
    dsa_ref,
    dsb_ref,
):
    even = is_even()

    @pl.when(pl.program_id(0) == 0)
    def _():
        for head in range(STEP):
            put_zeros(NEAR_ZEROS[0], 0, wa_ref.at[head], dsa_ref.at[head])
            put_zeros(NEAR_ZEROS[1], 0, wb_ref.at[head], dsb_ref.at[head])

    lay_near(even, 0, k_ref, inner_ref, pool_ref, near_ref, ka_ref, kb_ref)
    lay_near(even, 1, v_ref, inner_ref, pool_ref, near_ref, va_ref, vb_ref)
    keys, values, exps = (ka_ref, kb_ref), (va_ref, vb_ref), (pa_ref, pb_ref)
    weights, logits = (wa_ref, wb_ref), (dsa_ref, dsb_ref)
    grads = {}

    def differentiate(head, pair):
        score_grads(
            NEAR_CHUNKS[pair],
            NEAR_ADMIT[pair],
            values[pair].at[:, lanes_of(head)],
            two(even, g_ref, pair, head).T,
            stat_ref[head, 0:1, columns(pair)],
            stat_ref[head, 1:2, columns(pair)],
            exps[pair].at[head],
            weights[pair].at[head],
            logits[pair].at[head],
            0,
        )

    def multiply(head, pair):
        ds = logits[pair][head]
        cols = keys[pair][:, lanes_of(head)].T
        dq_t = (dqt_ref[head, :, columns(pair)] + mm(cols, ds)) * SCALE
        put_two(even, dq_ref, pair, head, dq_t.T)
        grads[head, pair] = (
            mm(ds, two(even, q_ref, pair, head)) * SCALE,
            mm(weights[pair][head], two(even, g_ref, pair, head)),
        )

    def collect(head, pair):
        if pair == 0:
            return
        lanes = lanes_of(head)
        for which, out in enumerate((kg_ref, vg_ref)):
            a = grads[head, 0][which]
            b = grads[head, 1][which]
            tokens = (a[:128], a[128:256] + b[:128], a[256:384] + b[128:256], b[256:384])
            halves = (b[576:640], b[704:768], a[384:448], a[448:512])
            for i in range(4):
                high = halves[i].astype(BF)
                low = (halves[i] - high.astype(F32)).astype(BF)
                spread = mm(spread_ref[...], jnp.concatenate([high, low], axis=0))
                out[block(even, i), lanes] = (tokens[i] + spread).astype(BF)
            near = jnp.concatenate([b[512:576], a[512:576]], axis=0).astype(BF)
            edge = jnp.concatenate([b[384:512], b[640:704], a[576:640] + b[768:832]], axis=0)
            innerg_ref[which, :, lanes] = (edge + mm(near_t_ref[...], near)).astype(BF)

    staggered(differentiate, multiply, collect)


CORE_VMEM = 32 * 2**20
SIDE_VMEM = 16 * 2**20


def params(limit=SIDE_VMEM):
    return pltpu.CompilerParams(vmem_limit_bytes=limit)


def cost(flops, moved):
    return pl.CostEstimate(flops=int(flops), bytes_accessed=int(moved), transcendentals=0)


def whole(shape):
    return pl.BlockSpec(shape, lambda i: (0,) * len(shape))


def part(rows, width, first=0):
    return pl.BlockSpec((rows, width), lambda i: (0, first + i))


def duo(rows, width, first=0):
    return pl.BlockSpec((2, rows, width), lambda i: (0, 0, first + i))


def per_head(rows, width, first=0):
    return pl.BlockSpec((STEP, rows, width), lambda i: (first + i, 0, 0))


def constant(matrix):
    return jnp.asarray(matrix, BF)


def shaped(*shape, dtype=BF):
    return jax.ShapeDtypeStruct(shape, dtype)


def swap_pairs(n):
    return [(i, i ^ 1) for i in range(n)]


def in_range(pairs, n):
    return [(i, j) for i, j in pairs if 0 <= j < n]


def cross_pairs(n):
    return in_range([(i, i + 1 if i % 2 else i - 1) for i in range(n)], n)


def far_pairs(n):
    return in_range([(i, i - 2 if i % 2 else i + 2) for i in range(n)], n)


def back_pairs(n):
    return in_range([(i, i + 2 if i % 2 else i - 2) for i in range(n)], n)


def call_pool(keys, values):
    tok, lanes = keys.shape
    width = 256
    return pl.pallas_call(
        pool_kernel,
        grid=(lanes // width,),
        in_specs=[part(tok, width), part(tok, width)],
        out_specs=[duo(EDGE, width), duo(EDGE, width), duo(64, width)],
        out_shape=[shaped(2, EDGE, lanes), shaped(2, EDGE, lanes), shaped(2, 64, lanes)],
        compiler_params=params(60 * 2**20),
        cost_estimate=cost(1e9, 5 * tok * lanes * 2),
        name="pool",
    )(keys, values)


def call_far(cross, far):
    lanes = cross.shape[2]
    width = lanes
    return pl.pallas_call(
        far_kernel,
        grid=(lanes // width,),
        in_specs=[whole((64, 256)), duo(EDGE, width), duo(64, width)],
        out_specs=duo(128, width),
        out_shape=shaped(2, 128, lanes),
        compiler_params=params(),
        cost_estimate=cost(1e9, 2 * 448 * lanes * 2),
        name="far",
    )(constant(FAR_POOL), cross, far)


def call_first(n, queries, keys, values, inner):
    tok, lanes = queries.shape
    heads = lanes // HD
    fixed = [constant(m) for m in (BLOCK_POOL, NEAR_POOL)]
    return pl.pallas_call(
        functools.partial(first_kernel, n),
        grid=(heads // STEP,),
        in_specs=[whole(m.shape) for m in fixed] + [part(tok, WIDE)] * 3 + [duo(EDGE, WIDE)],
        out_specs=[
            per_head(NEAR_ROWS[0], PAIR),
            per_head(NEAR_ROWS[1], PAIR),
            per_head(HD, tok),
            per_head(8, tok),
        ],
        out_shape=[
            shaped(heads, NEAR_ROWS[0], PAIR),
            shaped(heads, NEAR_ROWS[1], PAIR),
            shaped(heads, HD, tok, dtype=F32),
            shaped(heads, 8, tok, dtype=F32),
        ],
        scratch_shapes=[pltpu.VMEM((rows, WIDE), BF) for rows in NEAR_ROWS * 2]
        + [pltpu.VMEM((STEP, 2, NEAR_ROWS[1], PAIR), F32)],
        compiler_params=params(CORE_VMEM),
        cost_estimate=cost(heads * 1.5e9, 20 * tok * lanes),
        name="first",
    )(*fixed, queries, keys, values, inner)


def call_cross(n, queries, out_grad, cross, far, swap, sums, stats):
    tok, lanes = queries.shape
    heads = lanes // HD
    fixed = [constant(m) for m in (NEAR_POOL, NEAR_POOL.T)]
    return pl.pallas_call(
        functools.partial(cross_kernel, n),
        grid=(heads // STEP,),
        in_specs=[whole(m.shape) for m in fixed]
        + [part(tok, WIDE)] * 2
        + [duo(EDGE, WIDE), duo(64, WIDE), duo(128, WIDE), per_head(HD, tok), per_head(8, tok)],
        out_specs=[
            part(tok, WIDE),
            per_head(HD, tok),
            per_head(8, tok),
            duo(EDGE, WIDE),
            duo(64, WIDE),
            duo(128, WIDE),
        ],
        out_shape=[
            shaped(tok, lanes),
            shaped(heads, HD, tok, dtype=F32),
            shaped(heads, 8, tok, dtype=F32),
            shaped(2, EDGE, lanes),
            shaped(2, 64, lanes),
            shaped(2, 128, lanes),
        ],
        scratch_shapes=[
            pltpu.VMEM((CROSS_ROWS, WIDE), BF),
            pltpu.VMEM((CROSS_ROWS, WIDE), BF),
            pltpu.VMEM((STEP, 2, CROSS_ROWS, PAIR), F32),
            pltpu.VMEM((STEP, 2, 512, PAIR), BF),
            pltpu.VMEM((STEP, 2, 512, PAIR), BF),
        ],
        compiler_params=params(CORE_VMEM),
        cost_estimate=cost(heads * 1.5e9, 20 * tok * lanes),
        name="cross",
    )(*fixed, queries, out_grad, cross, far, swap, sums, stats)


def call_last(arrays, inner, pa, pb, stats, dqt, group, earlier):
    start, heads = group
    first = start // STEP
    tok, feat = arrays[0].shape
    lanes = heads * HD
    taken = [] if earlier is None else [earlier]
    fixed = [constant(m) for m in (BLOCK_POOL, NEAR_POOL, NEAR_POOL.T, BLOCK_SPREAD)]

    def kernel(*refs):
        last_kernel(*refs[:13], *refs[13 + len(taken) :])

    return pl.pallas_call(
        kernel,
        grid=(heads // STEP,),
        in_specs=[whole(m.shape) for m in fixed]
        + [part(tok, WIDE, first)] * 4
        + [
            duo(EDGE, WIDE, first),
            per_head(NEAR_ROWS[0], PAIR, first),
            per_head(NEAR_ROWS[1], PAIR, first),
            per_head(8, tok, first),
            per_head(HD, tok, first),
        ]
        + [pl.BlockSpec(memory_space=pl.ANY)] * len(taken),
        out_specs=[part(tok, WIDE, first), part(tok, WIDE), part(tok, WIDE), duo(EDGE, WIDE)],
        out_shape=[
            shaped(tok, feat, dtype=F32),
            shaped(tok, lanes),
            shaped(tok, lanes),
            shaped(2, EDGE, lanes),
        ],
        scratch_shapes=[pltpu.VMEM((rows, WIDE), BF) for rows in NEAR_ROWS * 2]
        + [pltpu.VMEM((STEP, rows, PAIR), BF) for rows in NEAR_ROWS * 2],
        input_output_aliases={13 + i: i for i in range(len(taken))},
        compiler_params=params(CORE_VMEM),
        cost_estimate=cost(heads * 1.5e9, 20 * tok * lanes),
        name="last",
    )(*fixed, *arrays, inner, pa, pb, stats, dqt, *taken)


def call_fold(cross, far, got):
    lanes = cross.shape[2]
    width = lanes
    return pl.pallas_call(
        fold_kernel,
        grid=(lanes // width,),
        in_specs=[whole((256, 64)), duo(EDGE, width), duo(64, width), duo(128, width)],
        out_specs=[duo(EDGE, width), duo(64, width)],
        out_shape=[shaped(2, EDGE, lanes), shaped(2, 64, lanes)],
        compiler_params=params(),
        cost_estimate=cost(1e9, 2 * 768 * lanes * 2),
        name="fold",
    )(constant(FAR_POOL.T), cross, far, got)


def call_final(cross, inner, far, kg, vg, feat, group, earlier):
    first, heads = group
    tok, lanes = kg.shape
    width = 256
    offset = first * HD // width
    taken = [] if earlier is None else list(earlier)

    def kernel(*refs):
        final_kernel(*refs[:6], *refs[6 + len(taken) :])

    return pl.pallas_call(
        kernel,
        grid=(lanes // width,),
        in_specs=[
            whole((512, 576)),
            duo(EDGE, width, offset),
            duo(EDGE, width),
            duo(64, width, offset),
        ]
        + [part(tok, width)] * 2
        + [pl.BlockSpec(memory_space=pl.ANY)] * len(taken),
        out_specs=[part(tok, width, offset)] * 2,
        out_shape=[shaped(tok, feat, dtype=F32)] * 2,
        input_output_aliases={6 + i: i for i in range(len(taken))},
        compiler_params=params(),
        cost_estimate=cost(2e9, 16 * tok * lanes),
        name="final",
    )(constant(SPREAD), cross, inner, far, kg, vg, *taken)


GROUPS = ((0, 4), (4, 4))


def body(queries, keys, values, out_grad):
    feat = queries.shape[1]
    n = lax.axis_size("ctx")
    send = functools.partial(lax.ppermute, axis_name="ctx")
    cross, inner, far = call_pool(keys, values)
    cross = send(cross, perm=cross_pairs(n))
    far = send(far, perm=far_pairs(n))
    inner = send(inner, perm=swap_pairs(n))
    pa, pb, sums, stats = call_first(n, queries, keys, values, inner)
    cross, far, stats = lax.optimization_barrier((cross, far, stats))
    swap = send(call_far(cross, far), perm=swap_pairs(n))
    att, dqt, stats, cross_g, far_g, swap_g = call_cross(
        n, queries, out_grad, cross, far, swap, sums, stats
    )
    cross_g, far_g = call_fold(cross_g, far_g, send(swap_g, perm=swap_pairs(n)))
    cross_g, far_g, stats = lax.optimization_barrier((cross_g, far_g, stats))
    cross_g = send(cross_g, perm=cross_pairs(n))
    far_g = send(far_g, perm=back_pairs(n))
    arrays = (queries, keys, values, out_grad)
    dq = None
    parts = []
    for number, group in enumerate(GROUPS):
        if number == 1:
            far_g, stats = lax.optimization_barrier((far_g, stats))
        dq, kg, vg, inner_g = call_last(arrays, inner, pa, pb, stats, dqt, group, dq)
        parts.append((send(inner_g, perm=swap_pairs(n)), kg, vg))
    grads = None
    for group, (inner_g, kg, vg) in zip(GROUPS, parts):
        grads = call_final(cross_g, inner_g, far_g, kg, vg, feat, group, grads)
    return att, dq, *grads


def solution(mesh):
    spec = P("ctx", None)
    return jax.shard_map(
        body,
        mesh=mesh,
        in_specs=(spec, spec, spec, spec),
        out_specs=(spec, spec, spec, spec),
        check_vma=False,
    )
```

```python
import functools
import math

import jax
import jax.numpy as jnp
import numpy as np
from jax import lax
from jax.experimental import pallas as pl
from jax.experimental.pallas import tpu as pltpu
from jax.sharding import PartitionSpec as P

HD = 128
NB = 128
PAIR = 2 * NB
EDGE = 2 * NB
SCALE = 1.0 / math.sqrt(HD)
SCALE_LOG2 = SCALE * math.log2(math.e)
PENALTY = 1e30
BF = jnp.bfloat16
F32 = jnp.float32


def pool_matrix(rows, source_rows, pieces):
    matrix = np.zeros((rows, source_rows), np.float32)
    for first, count, source, factor in pieces:
        for row in range(count):
            start = source + row * factor
            matrix[first + row, start : start + factor] = 1.0 / factor
    return matrix


BLOCK_POOL = pool_matrix(64, 128, [(0, 64, 0, 2)])
NEAR_POOL = pool_matrix(128, 256, [(0, 64, 0, 2), (64, 32, 0, 4), (96, 32, 128, 2)])
FAR_POOL = pool_matrix(64, 256, [(0, 16, 0, 8), (16, 16, 128, 4), (32, 32, 192, 2)])
BLOCK_SPREAD = np.concatenate([BLOCK_POOL.T, BLOCK_POOL.T], axis=1)


def mm(a, b):
    return jnp.dot(a, b, preferred_element_type=F32)


def mm_nt(a, b):
    return lax.dot_general(a, b, (((1,), (1,)), ((), ())), preferred_element_type=F32)


def is_even():
    return lax.rem(lax.axis_index("ctx"), 2) == 0


def block(even, number):
    return pl.ds(pl.multiple_of(jnp.where(even, number, 3 - number) * NB, NB), NB)


def means():
    row = lax.broadcasted_iota(jnp.int32, (NB, NB), 0)
    col = lax.broadcasted_iota(jnp.int32, (NB, NB), 1)
    matrix = jnp.where(row == (col >> 1), 0.5, 0.0)
    matrix = jnp.where(row == (col >> 2) + 64, 0.25, matrix)
    return jnp.where(row == (col >> 3) + 96, 0.125, matrix).astype(BF)


def pool_kernel(
    k_ref,
    v_ref,
    cross_out,
    inner_out,
    far_out,
    rows_ref,
    cross_ref,
    inner_ref,
    far_ref,
    sems,
    out_sems,
):
    even = is_even()

    def copy(which, b):
        ref = (k_ref, v_ref)[which]
        return pltpu.make_async_copy(
            ref.at[block(even, b), :], rows_ref.at[which, b], sems.at[which, b]
        )

    for which in range(2):
        for b in range(4):
            copy(which, b).start()
    matrix = means()
    copies = []
    for which in range(2):
        for b in range(4):
            copy(which, b).wait()
            rows = rows_ref[which, b]
            pooled = mm(matrix, rows).astype(BF)
            if b == 0:
                cross_ref[which, :128] = rows
                inner_ref[which, 192:224] = pooled[64:96]
            if b == 1:
                cross_ref[which, 128:192] = pooled[:64]
                inner_ref[which, 224:] = pooled[64:96]
            if b == 2:
                inner_ref[which, 128:192] = pooled[:64]
                cross_ref[which, 192:224] = pooled[64:96]
            if b == 3:
                inner_ref[which, :128] = rows
                cross_ref[which, 224:] = pooled[64:96]
            far_ref[which, b * 16 : (b + 1) * 16] = pooled[96:112]
        places = ((cross_ref, cross_out), (far_ref, far_out), (inner_ref, inner_out))
        for i, (source, target) in enumerate(places):
            out = pltpu.make_async_copy(
                source.at[which], target.at[which], out_sems.at[which, i]
            )
            out.start()
            copies.append(out)
    for out in copies:
        out.wait()


def far_kernel(pool_ref, cross_ref, far_ref, out_ref):
    for which in range(2):
        out_ref[which, :64] = far_ref[which]
        out_ref[which, 64:] = mm(pool_ref[...], cross_ref[which]).astype(BF)


def fold_kernel(pool_ref, cross_ref, far_ref, got_ref, cross_out, far_out):
    for which in range(2):
        spread = mm(pool_ref[...], got_ref[which, 64:])
        cross_out[which] = (cross_ref[which].astype(F32) + spread).astype(BF)
        far_out[which] = (far_ref[which].astype(F32) + got_ref[which, :64].astype(F32)).astype(BF)


def final_kernel(cross_ref, inner_ref, far_ref, kg_ref, vg_ref, kg_out, vg_out):
    even = is_even()
    row = lax.broadcasted_iota(jnp.int32, (NB, NB), 0)
    col = lax.broadcasted_iota(jnp.int32, (NB, NB), 1)
    matrix = jnp.where((row >> 1) == col, 0.5, 0.0)
    matrix = jnp.where((row >> 2) + 64 == col, 0.25, matrix)
    matrix = jnp.where((row >> 3) + 96 == col, 0.125, matrix).astype(BF)
    for which, (ref, out) in enumerate(((kg_ref, kg_out), (vg_ref, vg_out))):
        cross = cross_ref.at[which]
        inner = inner_ref.at[which]
        none = jnp.zeros((64, out.shape[1]), BF)
        firsts = (none, cross[128:192], inner[128:192], none)
        seconds = (inner[192:224], inner[224:], cross[192:224], cross[224:])
        for b in range(4):
            far = far_ref[which, b * 16 : (b + 1) * 16]
            pooled = jnp.concatenate([firsts[b], seconds[b], far, none[:16]], axis=0)
            total = ref[block(even, b), :].astype(F32) + mm(matrix, pooled)
            if b == 0:
                total = total + cross[:128].astype(F32)
            if b == 3:
                total = total + inner[:128].astype(F32)
            out[block(even, b), :] = total


NEAR_ROWS = (640, 832)
NEAR_CHUNKS = (
    ((0, 384, 0, "own"), (384, 512, 1, "own"), (512, 640, 2, "inner")),
    (
        (0, 384, 0, "own"),
        (384, 512, 0, "inner"),
        (512, 576, 1, "inner"),
        (576, 640, 1, "own"),
        (640, 704, 1, "inner"),
        (704, 768, 1, "own"),
        (768, 832, 2, "inner"),
    ),
)
NEAR_ADMIT = (
    (((0, 256), (384, 512), (512, 640)), ((0, 384), (448, 512), (512, 640))),
    (((0, 384), (512, 704), (768, 832)), ((128, 512), (576, 768), (768, 832))),
)
NEAR_ZEROS = (
    (((256, 384),), ((384, 448),)),
    (((384, 512), (704, 768)), ((0, 128), (512, 576))),
)
CROSS_ROWS = 640
CROSS_SPAN = ((0, 512), (256, 576))
CROSS_CHUNKS = (
    (
        (0, 128, 0, "cross"),
        (128, 192, 1, "cross"),
        (192, 256, 1, "cross"),
        (256, 320, 2, "cross"),
        (320, 384, 3, "far0"),
        (384, 448, 3, "far1"),
        (448, 512, 3, "far2"),
    ),
    (
        (256, 320, 2, "cross"),
        (320, 384, 3, "far0"),
        (384, 448, 3, "far1"),
        (448, 512, 3, "far2"),
        (512, 576, 2, "cross"),
    ),
)
CROSS_ADMIT = ((((0, 128), (192, 512)), ((128, 512),)), (((256, 576),), ((256, 576),)))
CROSS_ZEROS = ((((128, 192),), ((0, 128),)), ((), ()))


def overlap(chunk, ranges):
    for low, high in ranges:
        first, end = max(chunk[0], low), min(chunk[1], high)
        if first < end:
            return first, end
    return None


def fold_rows(x, op):
    return op(x.reshape(x.shape[0] // 8, 8, x.shape[1]), axis=0)


def lanes_of(blk):
    return slice(blk * NB, (blk + 1) * NB)


def penalties_of(devices):
    d = lax.axis_index("ctx")
    step = jnp.where(is_even(), 1, -1)

    def penalty(other):
        return jnp.where((other >= 0) & (other < devices), 0.0, PENALTY).astype(F32)

    return {
        "own": 0.0,
        "cross": penalty(d - step),
        "inner": penalty(d + step),
        "far0": penalty(d - 2 * step),
        "far1": penalty(d + 3 * step),
        "far2": penalty(d + 2 * step),
    }


def scores(chunks, admit, penalties, rows, q, s_ref):
    best = [None, None]
    for chunk in chunks:
        low, high, level, side = chunk
        s = mm_nt(rows[low:high], q)
        s_ref[low:high] = s
        for blk in range(2):
            part = overlap(chunk, admit[blk])
            if part is None:
                continue
            piece = s[part[0] - low : part[1] - low, lanes_of(blk)]
            top = fold_rows(piece, jnp.max) * SCALE_LOG2 + (level - penalties[side])
            best[blk] = top if best[blk] is None else jnp.maximum(best[blk], top)
    return jnp.concatenate([jnp.max(b, axis=0, keepdims=True) for b in best], axis=1)


def exponentials(chunks, admit, penalties, best, s_ref, p_ref, base):
    totals = []
    for blk in range(2):
        lanes = lanes_of(blk)
        total = jnp.zeros((8, NB), F32)
        for chunk in chunks:
            low, high, level, side = chunk
            part = overlap(chunk, admit[blk])
            if part is None:
                continue
            shift = best[:, lanes] - (level - penalties[side])
            prob = jnp.exp2(s_ref[part[0] : part[1], lanes] * SCALE_LOG2 - shift)
            total = total + fold_rows(prob, jnp.sum)
            p_ref[part[0] - base : part[1] - base, lanes] = prob.astype(BF)
        totals.append(jnp.sum(total, axis=0, keepdims=True))
    return jnp.concatenate(totals, axis=1)


def score_grads(chunks, admit, product, inverse, delta, exp_ref, p_ref, ds_ref, base):
    for chunk in chunks:
        low, high, level, side = chunk
        dp = product(low, high)
        for blk in range(2):
            lanes = lanes_of(blk)
            part = overlap(chunk, admit[blk])
            if part is None:
                continue
            here = slice(part[0] - base, part[1] - base)
            piece = dp[part[0] - low : part[1] - low, lanes]
            prob = exp_ref[here, lanes].astype(F32) * inverse[:, lanes]
            p_ref[here, lanes] = prob.astype(BF)
            ds_ref[here, lanes] = (prob * (piece - delta[:, lanes])).astype(BF)


def put_zeros(zeros, base, *refs):
    for ref in refs:
        for blk in range(2):
            for low, high in zeros[blk]:
                ref[low - base : high - base, lanes_of(blk)] = jnp.zeros((high - low, NB), BF)


def lay_near(even, which, own, inner_ref, pool_ref, near_ref, a, b):
    inner = inner_ref[which]
    near = mm(near_ref[...], inner).astype(BF)
    tokens = [own[block(even, i), :] for i in range(4)]
    halves = [mm(pool_ref[...], t).astype(BF) for t in tokens]
    a[:128] = tokens[0]
    a[128:256] = tokens[1]
    a[256:384] = tokens[2]
    a[384:448] = halves[2]
    a[448:512] = halves[3]
    a[512:576] = near[64:]
    a[576:640] = inner[192:]
    b[:128] = tokens[1]
    b[128:256] = tokens[2]
    b[256:384] = tokens[3]
    b[384:512] = inner[:128]
    b[512:576] = near[:64]
    b[576:640] = halves[0]
    b[640:704] = inner[128:192]
    b[704:768] = halves[1]
    b[768:832] = inner[192:]


STEP = 2
CROSS_STEP = 4


def units(step):
    return [(head, pair) for head in range(step) for pair in range(2)]


def two(even, ref, pair, head):
    lanes = lanes_of(head)
    return jnp.concatenate(
        [ref[block(even, 2 * pair), lanes], ref[block(even, 2 * pair + 1), lanes]], axis=0
    )


def put_two(even, ref, pair, head, rows):
    ref[block(even, 2 * pair), lanes_of(head)] = rows[:NB]
    ref[block(even, 2 * pair + 1), lanes_of(head)] = rows[NB:]


def staggered(work, *stages):
    for time in range(len(work) + len(stages) - 1):
        for lag, stage in enumerate(stages):
            if 0 <= time - lag < len(work):
                stage(*work[time - lag])


def columns(pair):
    return slice(pair * PAIR, (pair + 1) * PAIR)


def first_kernel(
    devices,
    pool_ref,
    near_ref,
    q_ref,
    k_ref,
    v_ref,
    g_ref,
    inner_ref,
    pa_ref,
    pb_ref,
    dpa_ref,
    dpb_ref,
    ka_ref,
    kb_ref,
    out_ref,
    stat_ref,
    va_ref,
    vb_ref,
    s_ref,
):
    even = is_even()
    penalties = penalties_of(devices)
    lay_near(even, 0, k_ref, inner_ref, pool_ref, near_ref, ka_ref, kb_ref)
    lay_near(even, 1, v_ref, inner_ref, pool_ref, near_ref, va_ref, vb_ref)
    keys, values, exps = (ka_ref, kb_ref), (va_ref, vb_ref), (pa_ref, pb_ref)
    products = (dpa_ref, dpb_ref)
    best = {}

    def score(head, pair):
        best[head, pair] = scores(
            NEAR_CHUNKS[pair],
            NEAR_ADMIT[pair],
            penalties,
            keys[pair].at[:, lanes_of(head)],
            two(even, q_ref, pair, head),
            s_ref.at[head, pair],
        )

    def exponential(head, pair):
        p = exps[pair].at[head]
        put_zeros(NEAR_ZEROS[pair], 0, p)
        total = exponentials(
            NEAR_CHUNKS[pair],
            NEAR_ADMIT[pair],
            penalties,
            best[head, pair],
            s_ref.at[head, pair],
            p,
            0,
        )
        stat_ref[head, 0:1, columns(pair)] = best[head, pair]
        stat_ref[head, 1:2, columns(pair)] = total

    def product(head, pair):
        g_t = two(even, g_ref, pair, head).T
        for low, high, _, _ in NEAR_CHUNKS[pair]:
            dp = mm(values[pair][low:high, lanes_of(head)], g_t)
            products[pair][head, low:high] = dp.astype(BF)

    def attend(head, pair):
        cols = values[pair][:, lanes_of(head)].T
        out_ref[head, :, columns(pair)] = mm(cols, exps[pair][head])

    staggered(units(STEP), score, product, exponential, attend)


def cross_kernel(
    devices,
    near_ref,
    near_t_ref,
    q_ref,
    g_ref,
    cross_ref,
    far_ref,
    swap_ref,
    sum_ref,
    stat_ref,
    att_ref,
    dq_ref,
    stat_out,
    crossg_ref,
    farg_ref,
    swapg_ref,
    k_ref,
    v_ref,
    s_ref,
    p_ref,
    ds_ref,
):
    even = is_even()
    penalties = penalties_of(devices)

    @pl.when(pl.program_id(0) == 0)
    def _():
        for head, pair in units(CROSS_STEP):
            base = CROSS_SPAN[pair][0]
            put_zeros(CROSS_ZEROS[pair], base, p_ref.at[head, pair], ds_ref.at[head, pair])

    for which, rows in enumerate((k_ref, v_ref)):
        cross = cross_ref[which]
        near = mm(near_ref[...], cross).astype(BF)
        rows[:128] = cross[:128]
        rows[128:192] = near[:64]
        rows[192:256] = cross[128:192]
        rows[256:320] = cross[192:]
        rows[320:384] = far_ref[which]
        rows[384:512] = swap_ref[which]
        rows[512:576] = near[64:]
        rows[576:] = jnp.zeros((64, rows.shape[1]), BF)
    state = {}
    grads = {}

    def score(head, pair):
        best = scores(
            CROSS_CHUNKS[pair],
            CROSS_ADMIT[pair],
            penalties,
            k_ref.at[:, lanes_of(head)],
            two(even, q_ref, pair, head),
            s_ref.at[head, pair],
        )
        state[head, pair] = jnp.maximum(best, stat_ref[head, 0:1, columns(pair)])

    def exponential(head, pair):
        best = state[head, pair]
        total = exponentials(
            CROSS_CHUNKS[pair],
            CROSS_ADMIT[pair],
            penalties,
            best,
            s_ref.at[head, pair],
            p_ref.at[head, pair],
            CROSS_SPAN[pair][0],
        )
        factor = jnp.exp2(stat_ref[head, 0:1, columns(pair)] - best)
        inverse = 1.0 / (total + stat_ref[head, 1:2, columns(pair)] * factor)
        state[head, pair] = factor, inverse

    def attend(head, pair):
        base, end = CROSS_SPAN[pair]
        factor, inverse = state[head, pair]
        cols = v_ref[base:end, lanes_of(head)].T
        new = mm(cols, p_ref[head, pair, : end - base])
        out_t = (sum_ref[head, :, columns(pair)] * factor + new) * inverse
        put_two(even, att_ref, pair, head, out_t.T.astype(BF))
        g_t = two(even, g_ref, pair, head).T
        delta = jnp.sum(out_t * g_t.astype(F32), axis=0, keepdims=True)
        stat_out[head, 0:1, columns(pair)] = inverse * factor
        stat_out[head, 1:2, columns(pair)] = delta
        state[head, pair] = inverse, delta, g_t

    def differentiate(head, pair):
        inverse, delta, g_t = state[head, pair]
        p = p_ref.at[head, pair]
        score_grads(
            CROSS_CHUNKS[pair],
            CROSS_ADMIT[pair],
            lambda low, high: mm(v_ref[low:high, lanes_of(head)], g_t),
            inverse,
            delta,
            p,
            p,
            ds_ref.at[head, pair],
            CROSS_SPAN[pair][0],
        )

    def multiply(head, pair):
        base, end = CROSS_SPAN[pair]
        ds = ds_ref[head, pair, : end - base]
        cols = k_ref[base:end, lanes_of(head)].T
        dq_ref[head, :, columns(pair)] = mm(cols, ds)
        grads[head, pair] = (
            mm(ds, two(even, q_ref, pair, head)) * SCALE,
            mm(p_ref[head, pair, : end - base], two(even, g_ref, pair, head)),
        )

    staggered(units(CROSS_STEP), score, exponential, attend, differentiate, multiply)
    for head in range(CROSS_STEP):
        lanes = lanes_of(head)
        for which in range(2):
            a = grads[head, 0][which]
            b = grads[head, 1][which]
            near = jnp.concatenate([a[128:192], b[256:320]], axis=0).astype(BF)
            edge = jnp.concatenate([a[:128], a[192:256], a[256:320] + b[:64]], axis=0)
            crossg_ref[which, :, lanes] = (edge + mm(near_t_ref[...], near)).astype(BF)
            far = (a[320:512] + b[64:256]).astype(BF)
            farg_ref[which, :, lanes] = far[:64]
            swapg_ref[which, :, lanes] = far[64:]


def last_kernel(
    near_t_ref,
    spread_ref,
    q_ref,
    g_ref,
    pa_ref,
    pb_ref,
    dpa_ref,
    dpb_ref,
    ka_ref,
    kb_ref,
    stat_ref,
    dqt_ref,
    dq_ref,
    kg_ref,
    vg_ref,
    innerg_ref,
    wa_ref,
    wb_ref,
    dsa_ref,
    dsb_ref,
):
    even = is_even()

    @pl.when(pl.program_id(0) == 0)
    def _():
        for head in range(STEP):
            put_zeros(NEAR_ZEROS[0], 0, wa_ref.at[head], dsa_ref.at[head])
            put_zeros(NEAR_ZEROS[1], 0, wb_ref.at[head], dsb_ref.at[head])

    keys, exps, products = (ka_ref, kb_ref), (pa_ref, pb_ref), (dpa_ref, dpb_ref)
    weights, logits = (wa_ref, wb_ref), (dsa_ref, dsb_ref)
    grads = {}

    def differentiate(head, pair):
        score_grads(
            NEAR_CHUNKS[pair],
            NEAR_ADMIT[pair],
            lambda low, high: products[pair][head, low:high].astype(F32),
            stat_ref[head, 0:1, columns(pair)],
            stat_ref[head, 1:2, columns(pair)],
            exps[pair].at[head],
            weights[pair].at[head],
            logits[pair].at[head],
            0,
        )

    def multiply(head, pair):
        ds = logits[pair][head]
        cols = keys[pair][:, lanes_of(head)].T
        dq_t = (dqt_ref[head, :, columns(pair)] + mm(cols, ds)) * SCALE
        put_two(even, dq_ref, pair, head, dq_t.T)
        grads[head, pair] = (
            mm(ds, two(even, q_ref, pair, head)) * SCALE,
            mm(weights[pair][head], two(even, g_ref, pair, head)),
        )

    def collect(head, pair):
        if pair == 0:
            return
        lanes = lanes_of(head)
        for which, out in enumerate((kg_ref, vg_ref)):
            a = grads[head, 0][which]
            b = grads[head, 1][which]
            tokens = (a[:128], a[128:256] + b[:128], a[256:384] + b[128:256], b[256:384])
            halves = (b[576:640], b[704:768], a[384:448], a[448:512])
            for i in range(4):
                high = halves[i].astype(BF)
                low = (halves[i] - high.astype(F32)).astype(BF)
                spread = mm(spread_ref[...], jnp.concatenate([high, low], axis=0))
                out[block(even, i), lanes] = (tokens[i] + spread).astype(BF)
            near = jnp.concatenate([b[512:576], a[512:576]], axis=0).astype(BF)
            edge = jnp.concatenate([b[384:512], b[640:704], a[576:640] + b[768:832]], axis=0)
            innerg_ref[which, :, lanes] = (edge + mm(near_t_ref[...], near)).astype(BF)

    staggered(units(STEP), differentiate, multiply, collect)


SIDE_VMEM = 8 * 2**20


def params(limit=SIDE_VMEM):
    return pltpu.CompilerParams(vmem_limit_bytes=limit)


def cost(flops, moved):
    return pl.CostEstimate(flops=int(flops), bytes_accessed=int(moved), transcendentals=0)


def whole(shape):
    return pl.BlockSpec(shape, lambda i: (0,) * len(shape))


def part(rows, width, first=0):
    return pl.BlockSpec((rows, width), lambda i: (0, first + i))


def duo(rows, width, first=0):
    return pl.BlockSpec((2, rows, width), lambda i: (0, 0, first + i))


def per_head(rows, width, first=0, step=STEP):
    return pl.BlockSpec((step, rows, width), lambda i: (first + i, 0, 0))


def constant(matrix):
    return jnp.asarray(matrix, BF)


def shaped(*shape, dtype=BF):
    return jax.ShapeDtypeStruct(shape, dtype)


def swap_pairs(n):
    return [(i, i ^ 1) for i in range(n)]


def in_range(pairs, n):
    return [(i, j) for i, j in pairs if 0 <= j < n]


def cross_pairs(n):
    return in_range([(i, i + 1 if i % 2 else i - 1) for i in range(n)], n)


def far_pairs(n):
    return in_range([(i, i - 2 if i % 2 else i + 2) for i in range(n)], n)


def back_pairs(n):
    return in_range([(i, i + 2 if i % 2 else i - 2) for i in range(n)], n)


def call_pool(keys, values):
    tok, lanes = keys.shape
    return pl.pallas_call(
        pool_kernel,
        grid=(1,),
        in_specs=[pl.BlockSpec(memory_space=pl.ANY)] * 2,
        out_specs=[pl.BlockSpec(memory_space=pl.ANY)] * 3,
        out_shape=[shaped(2, EDGE, lanes), shaped(2, EDGE, lanes), shaped(2, 64, lanes)],
        scratch_shapes=[
            pltpu.VMEM((2, 4, NB, lanes), BF),
            pltpu.VMEM((2, EDGE, lanes), BF),
            pltpu.VMEM((2, EDGE, lanes), BF),
            pltpu.VMEM((2, 64, lanes), BF),
            pltpu.SemaphoreType.DMA((2, 4)),
            pltpu.SemaphoreType.DMA((2, 3)),
        ],
        compiler_params=params(60 * 2**20),
        cost_estimate=cost(1e9, 5 * tok * lanes * 2),
        name="pool",
    )(keys, values)


def call_far(cross, far):
    lanes = cross.shape[2]
    width = lanes
    return pl.pallas_call(
        far_kernel,
        grid=(lanes // width,),
        in_specs=[whole((64, 256)), duo(EDGE, width), duo(64, width)],
        out_specs=duo(128, width),
        out_shape=shaped(2, 128, lanes),
        compiler_params=params(),
        cost_estimate=cost(1e9, 2 * 448 * lanes * 2),
        name="far",
    )(constant(FAR_POOL), cross, far)


def call_first(n, arrays, inner):
    tok, lanes = arrays[0].shape
    heads = lanes // HD
    wide = STEP * HD
    fixed = [constant(m) for m in (BLOCK_POOL, NEAR_POOL)]
    return pl.pallas_call(
        functools.partial(first_kernel, n),
        grid=(heads // STEP,),
        in_specs=[whole(m.shape) for m in fixed] + [part(tok, wide)] * 4 + [duo(EDGE, wide)],
        out_specs=[per_head(rows, PAIR) for rows in NEAR_ROWS * 2]
        + [part(rows, wide) for rows in NEAR_ROWS]
        + [per_head(HD, tok), per_head(8, tok)],
        out_shape=[shaped(heads, rows, PAIR) for rows in NEAR_ROWS * 2]
        + [shaped(rows, lanes) for rows in NEAR_ROWS]
        + [shaped(heads, HD, tok, dtype=F32), shaped(heads, 8, tok, dtype=F32)],
        scratch_shapes=[pltpu.VMEM((rows, wide), BF) for rows in NEAR_ROWS]
        + [pltpu.VMEM((STEP, 2, NEAR_ROWS[1], PAIR), F32)],
        compiler_params=params(16 * 2**20),
        cost_estimate=cost(heads * 3e8, 4 * tok * lanes),
        name="first",
    )(*fixed, *arrays, inner)


def call_cross(n, queries, out_grad, cross, far, swap, sums, stats):
    tok, lanes = queries.shape
    heads = lanes // HD
    wide = CROSS_STEP * HD
    fixed = [constant(m) for m in (NEAR_POOL, NEAR_POOL.T)]
    return pl.pallas_call(
        functools.partial(cross_kernel, n),
        grid=(heads // CROSS_STEP,),
        in_specs=[whole(m.shape) for m in fixed]
        + [part(tok, wide)] * 2
        + [duo(EDGE, wide), duo(64, wide), duo(128, wide), per_head(HD, tok, step=CROSS_STEP), per_head(8, tok, step=CROSS_STEP)],
        out_specs=[
            part(tok, wide),
            per_head(HD, tok, step=CROSS_STEP),
            per_head(8, tok, step=CROSS_STEP),
            duo(EDGE, wide),
            duo(64, wide),
            duo(128, wide),
        ],
        out_shape=[
            shaped(tok, lanes),
            shaped(heads, HD, tok, dtype=F32),
            shaped(heads, 8, tok, dtype=F32),
            shaped(2, EDGE, lanes),
            shaped(2, 64, lanes),
            shaped(2, 128, lanes),
        ],
        scratch_shapes=[
            pltpu.VMEM((CROSS_ROWS, wide), BF),
            pltpu.VMEM((CROSS_ROWS, wide), BF),
            pltpu.VMEM((CROSS_STEP, 2, CROSS_ROWS, PAIR), F32),
            pltpu.VMEM((CROSS_STEP, 2, 512, PAIR), BF),
            pltpu.VMEM((CROSS_STEP, 2, 512, PAIR), BF),
        ],
        compiler_params=params(20 * 2**20),
        cost_estimate=cost(heads * 1.5e9, 20 * tok * lanes),
        name="cross",
    )(*fixed, queries, out_grad, cross, far, swap, sums, stats)


def call_last(queries, out_grad, near, stats, dqt, group, earlier):
    start, heads = group
    tok, feat = queries.shape
    first, wide, lanes = start // STEP, STEP * HD, heads * HD
    taken = [] if earlier is None else [earlier]
    fixed = [constant(m) for m in (NEAR_POOL.T, BLOCK_SPREAD)]

    def kernel(*refs):
        last_kernel(*refs[:12], *refs[12 + len(taken) :])

    return pl.pallas_call(
        kernel,
        grid=(heads // STEP,),
        in_specs=[whole(m.shape) for m in fixed]
        + [part(tok, wide, first)] * 2
        + [per_head(rows, PAIR, first) for rows in NEAR_ROWS * 2]
        + [part(rows, wide, first) for rows in NEAR_ROWS]
        + [per_head(8, tok, first), per_head(HD, tok, first)]
        + [pl.BlockSpec(memory_space=pl.ANY)] * len(taken),
        out_specs=[part(tok, wide, first), part(tok, wide), part(tok, wide), duo(EDGE, wide)],
        out_shape=[
            shaped(tok, feat, dtype=F32),
            shaped(tok, lanes),
            shaped(tok, lanes),
            shaped(2, EDGE, lanes),
        ],
        scratch_shapes=[pltpu.VMEM((STEP, rows, PAIR), BF) for rows in NEAR_ROWS * 2],
        input_output_aliases={12 + i: i for i in range(len(taken))},
        compiler_params=params(14 * 2**20),
        cost_estimate=cost(heads * 1.5e9, 20 * tok * lanes),
        name="last",
    )(*fixed, queries, out_grad, *near, stats, dqt, *taken)


def call_fold(cross, far, got):
    lanes = cross.shape[2]
    width = lanes
    return pl.pallas_call(
        fold_kernel,
        grid=(lanes // width,),
        in_specs=[whole((256, 64)), duo(EDGE, width), duo(64, width), duo(128, width)],
        out_specs=[duo(EDGE, width), duo(64, width)],
        out_shape=[shaped(2, EDGE, lanes), shaped(2, 64, lanes)],
        compiler_params=params(),
        cost_estimate=cost(1e9, 2 * 768 * lanes * 2),
        name="fold",
    )(constant(FAR_POOL.T), cross, far, got)


def call_final(cross, inner, far, kg, vg, feat, group, earlier):
    first, heads = group
    tok, lanes = kg.shape
    width = min(512, lanes)
    offset = first * HD // width
    taken = [] if earlier is None else list(earlier)

    def kernel(*refs):
        final_kernel(*refs[:5], *refs[5 + len(taken) :])

    return pl.pallas_call(
        kernel,
        grid=(lanes // width,),
        in_specs=[
            duo(EDGE, width, offset),
            duo(EDGE, width),
            duo(64, width, offset),
        ]
        + [part(tok, width)] * 2
        + [pl.BlockSpec(memory_space=pl.ANY)] * len(taken),
        out_specs=[part(tok, width, offset)] * 2,
        out_shape=[shaped(tok, feat, dtype=F32)] * 2,
        input_output_aliases={5 + i: i for i in range(len(taken))},
        compiler_params=params(),
        cost_estimate=cost(2e9, 16 * tok * lanes),
        name="final",
    )(cross, inner, far, kg, vg, *taken)


GROUPS = ((0, 4), (4, 4))


def body(queries, keys, values, out_grad):
    feat = queries.shape[1]
    n = lax.axis_size("ctx")
    send = functools.partial(lax.ppermute, axis_name="ctx")
    cross, inner, far = call_pool(keys, values)
    far = send(far, perm=far_pairs(n))
    inner = send(inner, perm=swap_pairs(n))
    cross = send(cross, perm=cross_pairs(n))
    arrays = (queries, keys, values, out_grad)
    *near, sums, stats = call_first(n, arrays, inner)
    cross, far, stats = lax.optimization_barrier((cross, far, stats))
    swap = send(call_far(cross, far), perm=swap_pairs(n))
    att, dqt, stats, cross_g, far_g, swap_g = call_cross(
        n, queries, out_grad, cross, far, swap, sums, stats
    )
    cross_g, far_g = call_fold(cross_g, far_g, send(swap_g, perm=swap_pairs(n)))
    cross_g, far_g, stats = lax.optimization_barrier((cross_g, far_g, stats))
    cross_g = send(cross_g, perm=cross_pairs(n))
    far_g = send(far_g, perm=back_pairs(n))
    dq = None
    parts = []
    for number, group in enumerate(GROUPS):
        if number == 1:
            far_g, stats = lax.optimization_barrier((far_g, stats))
        dq, kg, vg, inner_g = call_last(queries, out_grad, near, stats, dqt, group, dq)
        parts.append((send(inner_g, perm=swap_pairs(n)), kg, vg))
    grads = None
    for group, (inner_g, kg, vg) in zip(GROUPS, parts):
        grads = call_final(cross_g, inner_g, far_g, kg, vg, feat, group, grads)
    return att, dq, *grads


def solution(mesh):
    spec = P("ctx", None)
    return jax.shard_map(
        body,
        mesh=mesh,
        in_specs=(spec, spec, spec, spec),
        out_specs=(spec, spec, spec, spec),
        check_vma=False,
    )
```

```python
import functools
import math

import jax
import jax.numpy as jnp
import numpy as np
from jax import lax
from jax.experimental import pallas as pl
from jax.experimental.pallas import tpu as pltpu
from jax.sharding import PartitionSpec as P

HD = 128
NB = 128
PAIR = 2 * NB
EDGE = 2 * NB
SCALE = 1.0 / math.sqrt(HD)
SCALE_LOG2 = SCALE * math.log2(math.e)
PENALTY = 1e30
BF = jnp.bfloat16
F32 = jnp.float32


def pool_matrix(rows, source_rows, pieces):
    matrix = np.zeros((rows, source_rows), np.float32)
    for first, count, source, factor in pieces:
        for row in range(count):
            start = source + row * factor
            matrix[first + row, start : start + factor] = 1.0 / factor
    return matrix


BLOCK_POOL = pool_matrix(64, 128, [(0, 64, 0, 2)])
NEAR_POOL = pool_matrix(128, 256, [(0, 64, 0, 2), (64, 32, 0, 4), (96, 32, 128, 2)])
FAR_POOL = pool_matrix(64, 256, [(0, 16, 0, 8), (16, 16, 128, 4), (32, 32, 192, 2)])
BLOCK_SPREAD = np.concatenate([BLOCK_POOL.T, BLOCK_POOL.T], axis=1)


def mm(a, b):
    return jnp.dot(a, b, preferred_element_type=F32)


def mm_nt(a, b):
    return lax.dot_general(a, b, (((1,), (1,)), ((), ())), preferred_element_type=F32)


def is_even():
    return lax.rem(lax.axis_index("ctx"), 2) == 0


def block(even, number):
    return pl.ds(pl.multiple_of(jnp.where(even, number, 3 - number) * NB, NB), NB)


def means():
    row = lax.broadcasted_iota(jnp.int32, (NB, NB), 0)
    col = lax.broadcasted_iota(jnp.int32, (NB, NB), 1)
    matrix = jnp.where(row == (col >> 1), 0.5, 0.0)
    matrix = jnp.where(row == (col >> 2) + 64, 0.25, matrix)
    return jnp.where(row == (col >> 3) + 96, 0.125, matrix).astype(BF)


def pool_kernel(
    k_ref,
    v_ref,
    cross_out,
    inner_out,
    far_out,
    rows_ref,
    cross_ref,
    inner_ref,
    far_ref,
    sems,
    out_sems,
    raw_sems,
):
    even = is_even()

    def copy(which, b):
        ref = (k_ref, v_ref)[which]
        return pltpu.make_async_copy(
            ref.at[block(even, b), :], rows_ref.at[which, b], sems.at[which, b]
        )

    for which in range(2):
        for b in range(4):
            copy(which, b).start()
    matrix = means()
    copies = []
    for which in range(2):
        for b in range(4):
            copy(which, b).wait()
            rows = rows_ref[which, b]
            pooled = mm(matrix, rows).astype(BF)
            if b == 0:
                inner_ref[which, 64:96] = pooled[64:96]
            if b == 1:
                cross_ref[which, :64] = pooled[:64]
                inner_ref[which, 96:] = pooled[64:96]
            if b == 2:
                inner_ref[which, :64] = pooled[:64]
                cross_ref[which, 64:96] = pooled[64:96]
            if b == 3:
                cross_ref[which, 96:] = pooled[64:96]
            far_ref[which, b * 16 : (b + 1) * 16] = pooled[96:112]
            if b in (0, 3):
                target = (cross_out if b == 0 else inner_out).at[which, :NB]
                out = pltpu.make_async_copy(rows_ref.at[which, b], target, raw_sems.at[which, b % 2])
                out.start()
                copies.append(out)
        places = (
            (cross_ref, cross_out.at[:, NB:]),
            (far_ref, far_out),
            (inner_ref, inner_out.at[:, NB:]),
        )
        for i, (source, target) in enumerate(places):
            out = pltpu.make_async_copy(
                source.at[which], target.at[which], out_sems.at[which, i]
            )
            out.start()
            copies.append(out)
    for out in copies:
        out.wait()


def far_kernel(pool_ref, cross_ref, far_ref, out_ref):
    for which in range(2):
        out_ref[which, :64] = far_ref[which]
        out_ref[which, 64:] = mm(pool_ref[...], cross_ref[which]).astype(BF)


def fold_kernel(pool_ref, cross_ref, far_ref, got_ref, cross_out, far_out):
    for which in range(2):
        spread = mm(pool_ref[...], got_ref[which, 64:])
        cross_out[which] = (cross_ref[which].astype(F32) + spread).astype(BF)
        far_out[which] = (far_ref[which].astype(F32) + got_ref[which, :64].astype(F32)).astype(BF)


def final_kernel(
    offset, cross_ref, inner_ref, far_ref, kg_ref, vg_ref, kg_out, vg_out, rows_ref, sems
):
    even = is_even()
    copies = []
    row = lax.broadcasted_iota(jnp.int32, (NB, NB), 0)
    col = lax.broadcasted_iota(jnp.int32, (NB, NB), 1)
    matrix = jnp.where((row >> 1) == col, 0.5, 0.0)
    matrix = jnp.where((row >> 2) + 64 == col, 0.25, matrix)
    matrix = jnp.where((row >> 3) + 96 == col, 0.125, matrix).astype(BF)
    for which, (ref, out) in enumerate(((kg_ref, kg_out), (vg_ref, vg_out))):
        cross = cross_ref.at[which]
        inner = inner_ref.at[which]
        none = jnp.zeros((64, ref.shape[1]), BF)
        firsts = (none, cross[128:192], inner[128:192], none)
        seconds = (inner[192:224], inner[224:], cross[192:224], cross[224:])
        for b in range(4):
            far = far_ref[which, b * 16 : (b + 1) * 16]
            pooled = jnp.concatenate([firsts[b], seconds[b], far, none[:16]], axis=0)
            total = ref[block(even, b), :].astype(F32) + mm(matrix, pooled)
            if b == 0:
                total = total + cross[:128].astype(F32)
            if b == 3:
                total = total + inner[:128].astype(F32)
            rows_ref[which, b] = total
            copy = pltpu.make_async_copy(
                rows_ref.at[which, b],
                out.at[block(even, b), pl.ds(offset, ref.shape[1])],
                sems.at[which, b],
            )
            copy.start()
            copies.append(copy)
    for copy in copies:
        copy.wait()


NEAR_ROWS = (640, 832)
NEAR_CHUNKS = (
    ((0, 384, 0, "own"), (384, 512, 1, "own"), (512, 640, 2, "inner")),
    (
        (0, 384, 0, "own"),
        (384, 512, 0, "inner"),
        (512, 576, 1, "inner"),
        (576, 640, 1, "own"),
        (640, 704, 1, "inner"),
        (704, 768, 1, "own"),
        (768, 832, 2, "inner"),
    ),
)
NEAR_ADMIT = (
    (((0, 256), (384, 512), (512, 640)), ((0, 384), (448, 512), (512, 640))),
    (((0, 384), (512, 704), (768, 832)), ((128, 512), (576, 768), (768, 832))),
)
NEAR_ZEROS = (
    (((256, 384),), ((384, 448),)),
    (((384, 512), (704, 768)), ((0, 128), (512, 576))),
)
CROSS_ROWS = 640
CROSS_SPAN = ((0, 512), (256, 576))
CROSS_CHUNKS = (
    (
        (0, 128, 0, "cross"),
        (128, 192, 1, "cross"),
        (192, 256, 1, "cross"),
        (256, 320, 2, "cross"),
        (320, 384, 3, "far0"),
        (384, 448, 3, "far1"),
        (448, 512, 3, "far2"),
    ),
    (
        (256, 320, 2, "cross"),
        (320, 384, 3, "far0"),
        (384, 448, 3, "far1"),
        (448, 512, 3, "far2"),
        (512, 576, 2, "cross"),
    ),
)
CROSS_ADMIT = ((((0, 128), (192, 512)), ((128, 512),)), (((256, 576),), ((256, 576),)))
CROSS_ZEROS = ((((128, 192),), ((0, 128),)), ((), ()))


def overlap(chunk, ranges):
    for low, high in ranges:
        first, end = max(chunk[0], low), min(chunk[1], high)
        if first < end:
            return first, end
    return None


def fold_rows(x, op):
    return op(x.reshape(x.shape[0] // 8, 8, x.shape[1]), axis=0)


def lanes_of(blk):
    return slice(blk * NB, (blk + 1) * NB)


def penalties_of(devices):
    d = lax.axis_index("ctx")
    step = jnp.where(is_even(), 1, -1)

    def penalty(other):
        return jnp.where((other >= 0) & (other < devices), 0.0, PENALTY).astype(F32)

    return {
        "own": 0.0,
        "cross": penalty(d - step),
        "inner": penalty(d + step),
        "far0": penalty(d - 2 * step),
        "far1": penalty(d + 3 * step),
        "far2": penalty(d + 2 * step),
    }


def scores(chunks, admit, penalties, rows, q, s_ref):
    best = [None, None]
    for chunk in chunks:
        low, high, level, side = chunk
        s = mm_nt(rows[low:high], q)
        s_ref[low:high] = s
        for blk in range(2):
            part = overlap(chunk, admit[blk])
            if part is None:
                continue
            piece = s[part[0] - low : part[1] - low, lanes_of(blk)]
            top = fold_rows(piece, jnp.max) * SCALE_LOG2 + (level - penalties[side])
            best[blk] = top if best[blk] is None else jnp.maximum(best[blk], top)
    return jnp.concatenate([jnp.max(b, axis=0, keepdims=True) for b in best], axis=1)


def exponentials(chunks, admit, penalties, best, s_ref, p_ref, base):
    totals = []
    for blk in range(2):
        lanes = lanes_of(blk)
        total = jnp.zeros((8, NB), F32)
        for chunk in chunks:
            low, high, level, side = chunk
            part = overlap(chunk, admit[blk])
            if part is None:
                continue
            shift = best[:, lanes] - (level - penalties[side])
            prob = jnp.exp2(s_ref[part[0] : part[1], lanes] * SCALE_LOG2 - shift)
            total = total + fold_rows(prob, jnp.sum)
            p_ref[part[0] - base : part[1] - base, lanes] = prob.astype(BF)
        totals.append(jnp.sum(total, axis=0, keepdims=True))
    return jnp.concatenate(totals, axis=1)


def score_grads(chunks, admit, product, inverse, delta, exp_ref, p_ref, ds_ref, base):
    for chunk in chunks:
        low, high, level, side = chunk
        dp = product(low, high)
        for blk in range(2):
            lanes = lanes_of(blk)
            part = overlap(chunk, admit[blk])
            if part is None:
                continue
            here = slice(part[0] - base, part[1] - base)
            piece = dp[part[0] - low : part[1] - low, lanes]
            prob = exp_ref[here, lanes].astype(F32) * inverse[:, lanes]
            p_ref[here, lanes] = prob.astype(BF)
            ds_ref[here, lanes] = (prob * (piece - delta[:, lanes])).astype(BF)


def put_zeros(zeros, base, *refs):
    for ref in refs:
        for blk in range(2):
            for low, high in zeros[blk]:
                ref[low - base : high - base, lanes_of(blk)] = jnp.zeros((high - low, NB), BF)


def lay_near(even, which, own, inner_ref, pool_ref, near_ref, a, b):
    inner = inner_ref[which]
    near = mm(near_ref[...], inner).astype(BF)
    tokens = [own[block(even, i), :] for i in range(4)]
    halves = [mm(pool_ref[...], t).astype(BF) for t in tokens]
    a[:128] = tokens[0]
    a[128:256] = tokens[1]
    a[256:384] = tokens[2]
    a[384:448] = halves[2]
    a[448:512] = halves[3]
    a[512:576] = near[64:]
    a[576:640] = inner[192:]
    b[:128] = tokens[1]
    b[128:256] = tokens[2]
    b[256:384] = tokens[3]
    b[384:512] = inner[:128]
    b[512:576] = near[:64]
    b[576:640] = halves[0]
    b[640:704] = inner[128:192]
    b[704:768] = halves[1]
    b[768:832] = inner[192:]


STEP = 2
CROSS_STEP = 4


def units(step):
    return [(head, pair) for head in range(step) for pair in range(2)]


def two(even, ref, pair, head):
    lanes = lanes_of(head)
    return jnp.concatenate(
        [ref[block(even, 2 * pair), lanes], ref[block(even, 2 * pair + 1), lanes]], axis=0
    )


def put_two(even, ref, pair, head, rows):
    ref[block(even, 2 * pair), lanes_of(head)] = rows[:NB]
    ref[block(even, 2 * pair + 1), lanes_of(head)] = rows[NB:]


def staggered(work, *stages):
    for time in range(len(work) + len(stages) - 1):
        for lag, stage in enumerate(stages):
            if 0 <= time - lag < len(work):
                stage(*work[time - lag])


def columns(pair):
    return slice(pair * PAIR, (pair + 1) * PAIR)


def first_kernel(
    devices,
    pool_ref,
    near_ref,
    q_ref,
    k_ref,
    v_ref,
    g_ref,
    inner_ref,
    pa_ref,
    pb_ref,
    dpa_ref,
    dpb_ref,
    ka_ref,
    kb_ref,
    out_ref,
    stat_ref,
    va_ref,
    vb_ref,
    s_ref,
):
    even = is_even()
    penalties = penalties_of(devices)
    lay_near(even, 0, k_ref, inner_ref, pool_ref, near_ref, ka_ref, kb_ref)
    lay_near(even, 1, v_ref, inner_ref, pool_ref, near_ref, va_ref, vb_ref)
    keys, values, exps = (ka_ref, kb_ref), (va_ref, vb_ref), (pa_ref, pb_ref)
    products = (dpa_ref, dpb_ref)
    best = {}

    def score(head, pair):
        best[head, pair] = scores(
            NEAR_CHUNKS[pair],
            NEAR_ADMIT[pair],
            penalties,
            keys[pair].at[:, lanes_of(head)],
            two(even, q_ref, pair, head),
            s_ref.at[head, pair],
        )

    def exponential(head, pair):
        p = exps[pair].at[head]
        put_zeros(NEAR_ZEROS[pair], 0, p)
        total = exponentials(
            NEAR_CHUNKS[pair],
            NEAR_ADMIT[pair],
            penalties,
            best[head, pair],
            s_ref.at[head, pair],
            p,
            0,
        )
        stat_ref[head, 0:1, columns(pair)] = best[head, pair]
        stat_ref[head, 1:2, columns(pair)] = total

    def product(head, pair):
        g_t = two(even, g_ref, pair, head).T
        for low, high, _, _ in NEAR_CHUNKS[pair]:
            dp = mm(values[pair][low:high, lanes_of(head)], g_t)
            products[pair][head, low:high] = dp.astype(BF)

    def attend(head, pair):
        cols = values[pair][:, lanes_of(head)].T
        out_ref[head, :, columns(pair)] = mm(cols, exps[pair][head])

    staggered(units(STEP), score, product, exponential, attend)


def cross_kernel(
    devices,
    near_ref,
    near_t_ref,
    q_ref,
    g_ref,
    cross_ref,
    far_ref,
    swap_ref,
    sum_ref,
    stat_ref,
    att_ref,
    dq_ref,
    stat_out,
    crossg_ref,
    farg_ref,
    swapg_ref,
    k_ref,
    v_ref,
    s_ref,
    p_ref,
    ds_ref,
):
    even = is_even()
    penalties = penalties_of(devices)

    @pl.when(pl.program_id(0) == 0)
    def _():
        for head, pair in units(CROSS_STEP):
            base = CROSS_SPAN[pair][0]
            put_zeros(CROSS_ZEROS[pair], base, p_ref.at[head, pair], ds_ref.at[head, pair])

    for which, rows in enumerate((k_ref, v_ref)):
        cross = cross_ref[which]
        near = mm(near_ref[...], cross).astype(BF)
        rows[:128] = cross[:128]
        rows[128:192] = near[:64]
        rows[192:256] = cross[128:192]
        rows[256:320] = cross[192:]
        rows[320:384] = far_ref[which]
        rows[384:512] = swap_ref[which]
        rows[512:576] = near[64:]
        rows[576:] = jnp.zeros((64, rows.shape[1]), BF)
    state = {}
    grads = {}

    def score(head, pair):
        best = scores(
            CROSS_CHUNKS[pair],
            CROSS_ADMIT[pair],
            penalties,
            k_ref.at[:, lanes_of(head)],
            two(even, q_ref, pair, head),
            s_ref.at[head, pair],
        )
        state[head, pair] = jnp.maximum(best, stat_ref[head, 0:1, columns(pair)])

    def exponential(head, pair):
        best = state[head, pair]
        total = exponentials(
            CROSS_CHUNKS[pair],
            CROSS_ADMIT[pair],
            penalties,
            best,
            s_ref.at[head, pair],
            p_ref.at[head, pair],
            CROSS_SPAN[pair][0],
        )
        factor = jnp.exp2(stat_ref[head, 0:1, columns(pair)] - best)
        inverse = 1.0 / (total + stat_ref[head, 1:2, columns(pair)] * factor)
        state[head, pair] = factor, inverse

    def attend(head, pair):
        base, end = CROSS_SPAN[pair]
        factor, inverse = state[head, pair]
        cols = v_ref[base:end, lanes_of(head)].T
        new = mm(cols, p_ref[head, pair, : end - base])
        out_t = (sum_ref[head, :, columns(pair)] * factor + new) * inverse
        put_two(even, att_ref, pair, head, out_t.T.astype(BF))
        g_t = two(even, g_ref, pair, head).T
        delta = jnp.sum(out_t * g_t.astype(F32), axis=0, keepdims=True)
        stat_out[head, 0:1, columns(pair)] = inverse * factor
        stat_out[head, 1:2, columns(pair)] = delta
        state[head, pair] = inverse, delta, g_t

    def differentiate(head, pair):
        inverse, delta, g_t = state[head, pair]
        p = p_ref.at[head, pair]
        score_grads(
            CROSS_CHUNKS[pair],
            CROSS_ADMIT[pair],
            lambda low, high: mm(v_ref[low:high, lanes_of(head)], g_t),
            inverse,
            delta,
            p,
            p,
            ds_ref.at[head, pair],
            CROSS_SPAN[pair][0],
        )

    def multiply(head, pair):
        base, end = CROSS_SPAN[pair]
        ds = ds_ref[head, pair, : end - base]
        cols = k_ref[base:end, lanes_of(head)].T
        dq_ref[head, :, columns(pair)] = mm(cols, ds)
        grads[head, pair] = (
            mm(ds, two(even, q_ref, pair, head)) * SCALE,
            mm(p_ref[head, pair, : end - base], two(even, g_ref, pair, head)),
        )

    staggered(units(CROSS_STEP), score, exponential, attend, differentiate, multiply)
    for head in range(CROSS_STEP):
        lanes = lanes_of(head)
        for which in range(2):
            a = grads[head, 0][which]
            b = grads[head, 1][which]
            near = jnp.concatenate([a[128:192], b[256:320]], axis=0).astype(BF)
            edge = jnp.concatenate([a[:128], a[192:256], a[256:320] + b[:64]], axis=0)
            crossg_ref[which, :, lanes] = (edge + mm(near_t_ref[...], near)).astype(BF)
            far = (a[320:512] + b[64:256]).astype(BF)
            farg_ref[which, :, lanes] = far[:64]
            swapg_ref[which, :, lanes] = far[64:]


def last_kernel(
    near_t_ref,
    spread_ref,
    q_ref,
    g_ref,
    pa_ref,
    pb_ref,
    dpa_ref,
    dpb_ref,
    ka_ref,
    kb_ref,
    stat_ref,
    dqt_ref,
    dq_ref,
    kg_ref,
    vg_ref,
    innerg_ref,
    wa_ref,
    wb_ref,
    dsa_ref,
    dsb_ref,
):
    even = is_even()

    @pl.when(pl.program_id(0) == 0)
    def _():
        for head in range(STEP):
            put_zeros(NEAR_ZEROS[0], 0, wa_ref.at[head], dsa_ref.at[head])
            put_zeros(NEAR_ZEROS[1], 0, wb_ref.at[head], dsb_ref.at[head])

    keys, exps, products = (ka_ref, kb_ref), (pa_ref, pb_ref), (dpa_ref, dpb_ref)
    weights, logits = (wa_ref, wb_ref), (dsa_ref, dsb_ref)
    grads = {}

    def differentiate(head, pair):
        score_grads(
            NEAR_CHUNKS[pair],
            NEAR_ADMIT[pair],
            lambda low, high: products[pair][head, low:high].astype(F32),
            stat_ref[head, 0:1, columns(pair)],
            stat_ref[head, 1:2, columns(pair)],
            exps[pair].at[head],
            weights[pair].at[head],
            logits[pair].at[head],
            0,
        )

    def multiply(head, pair):
        ds = logits[pair][head]
        cols = keys[pair][:, lanes_of(head)].T
        dq_t = (dqt_ref[head, :, columns(pair)] + mm(cols, ds)) * SCALE
        put_two(even, dq_ref, pair, head, dq_t.T)
        grads[head, pair] = (
            mm(ds, two(even, q_ref, pair, head)) * SCALE,
            mm(weights[pair][head], two(even, g_ref, pair, head)),
        )

    def collect(head, pair):
        if pair == 0:
            return
        lanes = lanes_of(head)
        for which, out in enumerate((kg_ref, vg_ref)):
            a = grads[head, 0][which]
            b = grads[head, 1][which]
            tokens = (a[:128], a[128:256] + b[:128], a[256:384] + b[128:256], b[256:384])
            halves = (b[576:640], b[704:768], a[384:448], a[448:512])
            for i in range(4):
                high = halves[i].astype(BF)
                low = (halves[i] - high.astype(F32)).astype(BF)
                spread = mm(spread_ref[...], jnp.concatenate([high, low], axis=0))
                out[block(even, i), lanes] = (tokens[i] + spread).astype(BF)
            near = jnp.concatenate([b[512:576], a[512:576]], axis=0).astype(BF)
            edge = jnp.concatenate([b[384:512], b[640:704], a[576:640] + b[768:832]], axis=0)
            innerg_ref[which, :, lanes] = (edge + mm(near_t_ref[...], near)).astype(BF)

    staggered(units(STEP), differentiate, multiply, collect)


SIDE_VMEM = 8 * 2**20


def params(limit=SIDE_VMEM):
    return pltpu.CompilerParams(vmem_limit_bytes=limit)


def cost(flops, moved):
    return pl.CostEstimate(flops=int(flops), bytes_accessed=int(moved), transcendentals=0)


def whole(shape):
    return pl.BlockSpec(shape, lambda i: (0,) * len(shape))


def part(rows, width, first=0):
    return pl.BlockSpec((rows, width), lambda i: (0, first + i))


def duo(rows, width, first=0):
    return pl.BlockSpec((2, rows, width), lambda i: (0, 0, first + i))


def per_head(rows, width, first=0, step=STEP):
    return pl.BlockSpec((step, rows, width), lambda i: (first + i, 0, 0))


def constant(matrix):
    return jnp.asarray(matrix, BF)


def shaped(*shape, dtype=BF):
    return jax.ShapeDtypeStruct(shape, dtype)


def swap_pairs(n):
    return [(i, i ^ 1) for i in range(n)]


def in_range(pairs, n):
    return [(i, j) for i, j in pairs if 0 <= j < n]


def cross_pairs(n):
    return in_range([(i, i + 1 if i % 2 else i - 1) for i in range(n)], n)


def far_pairs(n):
    return in_range([(i, i - 2 if i % 2 else i + 2) for i in range(n)], n)


def back_pairs(n):
    return in_range([(i, i + 2 if i % 2 else i - 2) for i in range(n)], n)


def call_pool(keys, values):
    tok, lanes = keys.shape
    return pl.pallas_call(
        pool_kernel,
        grid=(1,),
        in_specs=[pl.BlockSpec(memory_space=pl.ANY)] * 2,
        out_specs=[pl.BlockSpec(memory_space=pl.ANY)] * 3,
        out_shape=[shaped(2, EDGE, lanes), shaped(2, EDGE, lanes), shaped(2, 64, lanes)],
        scratch_shapes=[
            pltpu.VMEM((2, 4, NB, lanes), BF),
            pltpu.VMEM((2, NB, lanes), BF),
            pltpu.VMEM((2, NB, lanes), BF),
            pltpu.VMEM((2, 64, lanes), BF),
            pltpu.SemaphoreType.DMA((2, 4)),
            pltpu.SemaphoreType.DMA((2, 3)),
            pltpu.SemaphoreType.DMA((2, 2)),
        ],
        compiler_params=params(60 * 2**20),
        cost_estimate=cost(1e9, 5 * tok * lanes * 2),
        name="pool",
    )(keys, values)


def call_far(cross, far):
    lanes = cross.shape[2]
    width = lanes
    return pl.pallas_call(
        far_kernel,
        grid=(lanes // width,),
        in_specs=[whole((64, 256)), duo(EDGE, width), duo(64, width)],
        out_specs=duo(128, width),
        out_shape=shaped(2, 128, lanes),
        compiler_params=params(),
        cost_estimate=cost(1e9, 2 * 448 * lanes * 2),
        name="far",
    )(constant(FAR_POOL), cross, far)


def call_first(n, arrays, inner):
    tok, lanes = arrays[0].shape
    heads = lanes // HD
    wide = STEP * HD
    fixed = [constant(m) for m in (BLOCK_POOL, NEAR_POOL)]
    return pl.pallas_call(
        functools.partial(first_kernel, n),
        grid=(heads // STEP,),
        in_specs=[whole(m.shape) for m in fixed] + [part(tok, wide)] * 4 + [duo(EDGE, wide)],
        out_specs=[per_head(rows, PAIR) for rows in NEAR_ROWS * 2]
        + [part(rows, wide) for rows in NEAR_ROWS]
        + [per_head(HD, tok), per_head(8, tok)],
        out_shape=[shaped(heads, rows, PAIR) for rows in NEAR_ROWS * 2]
        + [shaped(rows, lanes) for rows in NEAR_ROWS]
        + [shaped(heads, HD, tok, dtype=F32), shaped(heads, 8, tok, dtype=F32)],
        scratch_shapes=[pltpu.VMEM((rows, wide), BF) for rows in NEAR_ROWS]
        + [pltpu.VMEM((STEP, 2, NEAR_ROWS[1], PAIR), F32)],
        compiler_params=params(16 * 2**20),
        cost_estimate=cost(heads * 3e8, 4 * tok * lanes),
        name="first",
    )(*fixed, *arrays, inner)


def call_cross(n, queries, out_grad, cross, far, swap, sums, stats):
    tok, lanes = queries.shape
    heads = lanes // HD
    wide = CROSS_STEP * HD
    fixed = [constant(m) for m in (NEAR_POOL, NEAR_POOL.T)]
    return pl.pallas_call(
        functools.partial(cross_kernel, n),
        grid=(heads // CROSS_STEP,),
        in_specs=[whole(m.shape) for m in fixed]
        + [part(tok, wide)] * 2
        + [duo(EDGE, wide), duo(64, wide), duo(128, wide), per_head(HD, tok, step=CROSS_STEP), per_head(8, tok, step=CROSS_STEP)],
        out_specs=[
            part(tok, wide),
            per_head(HD, tok, step=CROSS_STEP),
            per_head(8, tok, step=CROSS_STEP),
            duo(EDGE, wide),
            duo(64, wide),
            duo(128, wide),
        ],
        out_shape=[
            shaped(tok, lanes),
            shaped(heads, HD, tok, dtype=F32),
            shaped(heads, 8, tok, dtype=F32),
            shaped(2, EDGE, lanes),
            shaped(2, 64, lanes),
            shaped(2, 128, lanes),
        ],
        scratch_shapes=[
            pltpu.VMEM((CROSS_ROWS, wide), BF),
            pltpu.VMEM((CROSS_ROWS, wide), BF),
            pltpu.VMEM((CROSS_STEP, 2, CROSS_ROWS, PAIR), F32),
            pltpu.VMEM((CROSS_STEP, 2, 512, PAIR), BF),
            pltpu.VMEM((CROSS_STEP, 2, 512, PAIR), BF),
        ],
        compiler_params=params(20 * 2**20),
        cost_estimate=cost(heads * 1.5e9, 20 * tok * lanes),
        name="cross",
    )(*fixed, queries, out_grad, cross, far, swap, sums, stats)


def call_last(queries, out_grad, near, stats, dqt, group, earlier):
    start, heads = group
    tok, feat = queries.shape
    first, wide, lanes = start // STEP, STEP * HD, heads * HD
    taken = [] if earlier is None else [earlier]
    fixed = [constant(m) for m in (NEAR_POOL.T, BLOCK_SPREAD)]

    def kernel(*refs):
        last_kernel(*refs[:12], *refs[12 + len(taken) :])

    return pl.pallas_call(
        kernel,
        grid=(heads // STEP,),
        in_specs=[whole(m.shape) for m in fixed]
        + [part(tok, wide, first)] * 2
        + [per_head(rows, PAIR, first) for rows in NEAR_ROWS * 2]
        + [part(rows, wide, first) for rows in NEAR_ROWS]
        + [per_head(8, tok, first), per_head(HD, tok, first)]
        + [pl.BlockSpec(memory_space=pl.ANY)] * len(taken),
        out_specs=[part(tok, wide, first), part(tok, wide), part(tok, wide), duo(EDGE, wide)],
        out_shape=[
            shaped(tok, feat, dtype=F32),
            shaped(tok, lanes),
            shaped(tok, lanes),
            shaped(2, EDGE, lanes),
        ],
        scratch_shapes=[pltpu.VMEM((STEP, rows, PAIR), BF) for rows in NEAR_ROWS * 2],
        input_output_aliases={12 + i: i for i in range(len(taken))},
        compiler_params=params(14 * 2**20),
        cost_estimate=cost(heads * 1.5e9, 20 * tok * lanes),
        name="last",
    )(*fixed, queries, out_grad, *near, stats, dqt, *taken)


def call_fold(cross, far, got):
    lanes = cross.shape[2]
    width = lanes
    return pl.pallas_call(
        fold_kernel,
        grid=(lanes // width,),
        in_specs=[whole((256, 64)), duo(EDGE, width), duo(64, width), duo(128, width)],
        out_specs=[duo(EDGE, width), duo(64, width)],
        out_shape=[shaped(2, EDGE, lanes), shaped(2, 64, lanes)],
        compiler_params=params(),
        cost_estimate=cost(1e9, 2 * 768 * lanes * 2),
        name="fold",
    )(constant(FAR_POOL.T), cross, far, got)


def call_final(cross, inner, far, kg, vg, feat, group, earlier):
    first, heads = group
    tok, lanes = kg.shape
    taken = [] if earlier is None else list(earlier)

    def kernel(*refs):
        final_kernel(first * HD, *refs[:5], *refs[5 + len(taken) :])

    return pl.pallas_call(
        kernel,
        grid=(1,),
        in_specs=[
            duo(EDGE, lanes, first // heads),
            duo(EDGE, lanes),
            duo(64, lanes, first // heads),
        ]
        + [part(tok, lanes)] * 2
        + [pl.BlockSpec(memory_space=pl.ANY)] * len(taken),
        out_specs=[pl.BlockSpec(memory_space=pl.ANY)] * 2,
        out_shape=[shaped(tok, feat, dtype=F32)] * 2,
        scratch_shapes=[
            pltpu.VMEM((2, 4, NB, lanes), F32),
            pltpu.SemaphoreType.DMA((2, 4)),
        ],
        input_output_aliases={5 + i: i for i in range(len(taken))},
        compiler_params=params(),
        cost_estimate=cost(2e9, 16 * tok * lanes),
        name="final",
    )(cross, inner, far, kg, vg, *taken)


GROUPS = ((0, 4), (4, 4))


def body(queries, keys, values, out_grad):
    feat = queries.shape[1]
    n = lax.axis_size("ctx")
    send = functools.partial(lax.ppermute, axis_name="ctx")
    cross, inner, far = call_pool(keys, values)
    far = send(far, perm=far_pairs(n))
    inner = send(inner, perm=swap_pairs(n))
    cross = send(cross, perm=cross_pairs(n))
    arrays = (queries, keys, values, out_grad)
    *near, sums, stats = call_first(n, arrays, inner)
    cross, far, stats = lax.optimization_barrier((cross, far, stats))
    swap = send(call_far(cross, far), perm=swap_pairs(n))
    att, dqt, stats, cross_g, far_g, swap_g = call_cross(
        n, queries, out_grad, cross, far, swap, sums, stats
    )
    cross_g, far_g = call_fold(cross_g, far_g, send(swap_g, perm=swap_pairs(n)))
    cross_g, far_g, stats = lax.optimization_barrier((cross_g, far_g, stats))
    cross_g = send(cross_g, perm=cross_pairs(n))
    far_g = send(far_g, perm=back_pairs(n))
    dq = None
    parts = []
    for number, group in enumerate(GROUPS):
        if number == 1:
            far_g, stats = lax.optimization_barrier((far_g, stats))
        dq, kg, vg, inner_g = call_last(queries, out_grad, near, stats, dqt, group, dq)
        parts.append((send(inner_g, perm=swap_pairs(n)), kg, vg))
    grads = None
    for group, (inner_g, kg, vg) in zip(GROUPS, parts):
        grads = call_final(cross_g, inner_g, far_g, kg, vg, feat, group, grads)
    return att, dq, *grads


def solution(mesh):
    spec = P("ctx", None)
    return jax.shard_map(
        body,
        mesh=mesh,
        in_specs=(spec, spec, spec, spec),
        out_specs=(spec, spec, spec, spec),
        check_vma=False,
    )
```
